512 devices in a mesh: blk: 8 (over y, x_hi), grp: 64 (over z, x_lo, core).
Axes of the slice: x: 4 (x_hi: 2, x_lo: 2; x = x_hi * 2 + x_lo), y: 4, z: 16, core: 2. Of those that a mesh axis runs over, the one named last changes fastest.
Arguments:
- image_embed: bfloat16 [6144, 1152], P(('blk', 'grp')), may hold values from -1 to 1
- text_embed: bfloat16 [6144, 1152], P(('blk', 'grp')), may hold values from -1 to 1
- logit_scale: float32 [], replicated, may hold values from 4 to 10
- logit_bias: float32 [], replicated, may hold values from -6 to -2
Outputs:
- image_grad: float32 [6144, 1152], P(('blk', 'grp'))
- text_grad: float32 [6144, 1152], P(('blk', 'grp'))
The draws below stay inside these ranges and needn't reach their ends.
All inputs are finite; a program needn't handle non-finite values.
Results may differ from the reference program's by a relative error of at most 0.0055.
Values may be sent and summed in bfloat16 or wider, within the bound.
A program may use at most 64 MiB of HBM per device.

```python
import math
import jax
import jax.numpy as jnp
from jax import lax

D = 1152
PAIRS = 6144


def paired_part(key):
    return jax.random.normal(key, (PAIRS, D), jnp.float32)


def draw_image_embed(key, part):
    shared = paired_part(key)
    key = jax.random.fold_in(key, 11)
    first, second = jax.random.split(key, 2)
    own = jax.random.normal(first, (PAIRS, D), jnp.float32)
    scales = jnp.exp(jax.random.uniform(second, (PAIRS, 1), jnp.float32, math.log(0.01), math.log(0.1)))
    base = 0.8 * shared + 0.6 * own
    return jnp.clip(scales * base, -1.0, 1.0).astype(jnp.bfloat16)


def draw_text_embed(key, part):
    shared = paired_part(key)
    key = jax.random.fold_in(key, 23)
    first, second = jax.random.split(key, 2)
    own = jax.random.normal(first, (PAIRS, D), jnp.float32)
    scales = jnp.exp(jax.random.uniform(second, (PAIRS, 1), jnp.float32, math.log(0.01), math.log(0.1)))
    base = 0.7 * shared + 0.7 * own
    return jnp.clip(scales * base, -1.0, 1.0).astype(jnp.bfloat16)


def setup_inputs(seed: int = 0) -> dict:
    key_list = jax.random.split(jax.random.key(seed), 5)
    image_embed = draw_image_embed(jax.random.fold_in(key_list[4], 71), 0)
    text_embed = draw_text_embed(jax.random.fold_in(key_list[4], 71), 0)
    logit_scale = jnp.clip(jax.random.uniform(key_list[2], (), jnp.float32, 4.0, 10.0), 4.0, 10.0)
    logit_bias = jnp.clip(jax.random.uniform(key_list[3], (), jnp.float32, -6.0, -2.0), -6.0, -2.0)
    return {"image_embed": image_embed, "text_embed": text_embed, "logit_scale": logit_scale, "logit_bias": logit_bias}


EPS = 1e-06

def unit_rows(embed):
    values = embed.astype(jnp.float32)
    recip = lax.rsqrt(lax.optimization_barrier(jnp.sum(values * values, axis=1, keepdims=True)) + EPS)
    unit = values * recip
    return (unit, unit.astype(jnp.bfloat16), recip)

def back_norm(unit, recip, grad):
    return recip * (grad - unit * lax.optimization_barrier(jnp.sum(unit * grad, axis=1, keepdims=True)))

def reference(image_embed, text_embed, logit_scale, logit_bias):
    image_unit, image_half, image_recip = unit_rows(image_embed)
    text_unit, text_half, text_recip = unit_rows(text_embed)
    block = math.gcd(PAIRS, 512)
    columns = lax.broadcasted_iota(jnp.int32, (block, PAIRS), 1)
    row_base = lax.broadcasted_iota(jnp.int32, (block, PAIRS), 0)

    def visit(total, index):
        start = (index * block).astype(jnp.int32)
        rows = lax.dynamic_slice_in_dim(image_half, start, block, 0)
        logits = logit_scale * jnp.dot(rows, text_half.T, preferred_element_type=jnp.float32) + logit_bias
        coef = jnp.where(columns == row_base + start, -jax.nn.sigmoid(-logits), jax.nn.sigmoid(logits)).astype(jnp.bfloat16)
        grad = logit_scale * jnp.dot(coef, text_half, preferred_element_type=jnp.float32)
        total = total + logit_scale * jnp.dot(coef.T, rows, preferred_element_type=jnp.float32)
        return (total, grad)
    text_unit_grad, grads = lax.scan(visit, jnp.zeros((PAIRS, D), jnp.float32), jnp.arange(PAIRS // block, dtype=jnp.int32))
    image_unit_grad = grads.reshape(PAIRS, D)
    return (back_norm(image_unit, image_recip, image_unit_grad), back_norm(text_unit, text_recip, text_unit_grad))
```

```python
import jax
import jax.numpy as jnp
from jax import lax
from jax.experimental import pallas as pl
from jax.experimental.pallas import tpu as pltpu
from jax.sharding import PartitionSpec as P

EPS = 1e-06
MESH = pl.DeviceIdType.MESH
ROWS = 16
USED = 12
LANES = 128
MAIN = 7 * LANES
REST = 2 * LANES
F32 = jnp.float32
BF16 = jnp.bfloat16
AROUND = (3, 2, 1)


class Place:
    def __init__(self):
        blk, grp = lax.axis_index("blk"), lax.axis_index("grp")
        self.y = blk // 2
        self.z = grp // 4
        self.x = (blk % 2) * 2 + (grp // 2) % 2
        self.core = grp % 2

    def at(self, x, y, z, core):
        return (y * 2 + x // 2, z * 4 + (x % 2) * 2 + core)

    def other_core(self):
        return self.at(self.x, self.y, self.z, 1 - self.core)

    def text_plane(self, k):
        x = self.x + (k % 2) * (1 - 2 * (self.x % 2))
        y = self.y + (k // 2) * (1 - 2 * (self.y % 2))
        return self.at(x, y, self.z, self.core)

    def image_plane(self, k):
        x = (self.x + (k % 2) * (2 * (self.x % 2) + 3)) % 4
        y = (self.y + (k // 2) * (2 * (self.y % 2) + 3)) % 4
        return self.at(x, y, self.z, self.core)

    def text_z(self, k):
        z = self.z + (k % 2) * (1 - 2 * (self.z % 2)) + (k // 2) * (4 - 8 * ((self.z // 4) % 2))
        return self.at(self.x, self.y, z, self.core)

    def image_z(self, k):
        z = self.z + (k % 2) * (2 - 4 * ((self.z // 2) % 2)) + (k // 2) * (8 * ((self.z // 4) % 2) + 12)
        return self.at(self.x, self.y, z % 16, self.core)


def pieces_up(rest):
    low, high = rest[:, 0:8], rest[:, 8:16]
    low_up, high_up = pltpu.roll(low, 4, 1), pltpu.roll(high, 4, 1)
    parts = []
    for c in (slice(0, LANES), slice(LANES, REST)):
        parts += [low_up[:, :, c], low[:, :, c], high_up[:, :, c]]
    return jnp.concatenate(parts + [jnp.zeros_like(parts[0])], axis=2)


def pack(main, rest):
    pieces = pieces_up(rest)
    lower = lax.broadcasted_iota(jnp.int32, pieces.shape, 1) >= 4
    return jnp.concatenate([main[:, 0:8], jnp.where(lower, pieces, main[:, 8:16])], axis=1)


def unpack_rest(packed):
    under = packed[:, 8:16]
    up = pltpu.roll(under, 4, 1)
    lower = lax.broadcasted_iota(jnp.int32, under[:, :, 0:LANES].shape, 1) >= 4
    lows, highs = [], []
    for c in (0, 3):
        first, second, third = (slice((c + i) * LANES, (c + i + 1) * LANES) for i in range(3))
        lows.append(jnp.where(lower, under[:, :, second], up[:, :, first]))
        highs.append(jnp.where(lower, 0.0, up[:, :, third]))
    return jnp.concatenate(
        [jnp.concatenate(lows, axis=2), jnp.concatenate(highs, axis=2)], axis=1
    )


def dot(a, b, dims):
    return lax.dot_general(a, b, (dims, ((), ())), preferred_element_type=F32)


def kernel(
    scale_ref,
    bias_ref,
    image_hbm,
    text_hbm,
    image_out,
    text_out,
    raw,
    units,
    grads,
    texts,
    images,
    texts_rest,
    images_rest,
    image_coefs,
    text_coefs,
    text_terms,
    image_terms,
    text_plane_out,
    text_plane_in,
    image_plane_out,
    image_plane_in,
    text_z_out,
    text_z_in,
    image_z_out,
    image_z_in,
    load_sems,
    send_sems,
    text_z_recv,
    text_plane_recv,
    image_z_recv,
    image_plane_recv,
    text_core_recv,
    image_core_recv,
    text_back_recv,
    image_back_recv,
    last_recv,
):
    loads = [
        pltpu.make_async_copy(image_hbm, raw.at[0], load_sems.at[0]),
        pltpu.make_async_copy(text_hbm, raw.at[1], load_sems.at[1]),
    ]
    for one in loads:
        one.start()
    place = Place()
    partner = place.other_core()
    text_plane, image_plane, image_z, text_z = (
        {k: way(k) for k in AROUND} for way in (place.text_plane, place.image_plane, place.image_z, place.text_z)
    )
    barrier = pltpu.get_barrier_semaphore()
    for k in AROUND:
        for device in (text_z[k], image_z[k], text_plane[k], image_plane[k]):
            pl.semaphore_signal(barrier, inc=1, device_id=device, device_id_type=MESH)
    pl.semaphore_signal(barrier, inc=1, device_id=partner, device_id_type=MESH)
    units[...] = jnp.zeros_like(units)
    for one in loads:
        one.wait()
    values = raw[...].astype(F32)
    recip = lax.rsqrt(jnp.sum(values * values, axis=2, keepdims=True) + EPS)
    units[:, 0:USED] = values * recip
    own = units[...]
    own_rest = own[:, :, MAIN:]
    own_packed = pack(own[:, :, :MAIN], own_rest).astype(BF16)
    images[0, 0, 0] = own_packed[0]
    texts[0, 0, 0] = own_packed[1]
    pl.semaphore_wait(barrier, 13)

    def remote(src, dst, send, recv, device):
        return pltpu.make_async_remote_copy(
            src_ref=src,
            dst_ref=dst,
            send_sem=send_sems.at[send],
            recv_sem=recv,
            device_id=device,
            device_id_type=MESH,
        )

    def arrived(ref, recv):
        remote(ref, ref, 0, recv, partner).wait_recv()

    def left(ref, send):
        remote(ref, ref, send, text_core_recv.at[0], partner).wait_send()

    def spread(blocks, plane, send, recv, dz):
        for k in AROUND:
            remote(blocks.at[0, dz, 0], blocks.at[0, dz, k], send, recv.at[dz], plane[k]).start()

    def complete(blocks, rests, plane_recv, send, core_recv, dz):
        arrived(blocks.at[0, dz, pl.ds(1, 3)], plane_recv.at[dz])
        remote(blocks.at[0, dz], blocks.at[1, dz], send, core_recv.at[dz], partner).start()
        rests[0, dz] = unpack_rest(blocks[0, dz].astype(F32)).astype(BF16)

    def partner_complete(blocks, rests, core_recv, dz):
        arrived(blocks.at[1, dz], core_recv.at[dz])
        rests[1, dz] = unpack_rest(blocks[1, dz].astype(F32)).astype(BF16)

    for k in AROUND:
        remote(texts.at[0, 0, 0], texts.at[0, k, 0], 0, text_z_recv.at[k], text_z[k]).start()
    for k in AROUND:
        remote(images.at[0, 0, 0], images.at[0, k, 0], 2, image_z_recv.at[k], image_z[k]).start()
    spread(texts, text_plane, 1, text_plane_recv, 0)
    spread(images, image_plane, 3, image_plane_recv, 0)
    for dz in (1, 2, 3):
        arrived(texts.at[0, dz, 0], text_z_recv.at[dz])
        spread(texts, text_plane, 1, text_plane_recv, dz)
        arrived(images.at[0, dz, 0], image_z_recv.at[dz])
        spread(images, image_plane, 3, image_plane_recv, dz)
    for dz in range(4):
        complete(texts, texts_rest, text_plane_recv, 4, text_core_recv, dz)
        complete(images, images_rest, image_plane_recv, 5, image_core_recv, dz)

    scale, bias = scale_ref[()], bias_ref[()]
    half = 16 * ROWS
    across = ((1,), (1,))

    def flat(ref, lane):
        return ref[lane].reshape(half, ref.shape[-1])

    def coefficients(rows, cols, col_lane):
        logits = dot(flat(rows[0], 0), flat(cols[0], col_lane), across)
        logits = logits + dot(flat(rows[1], 0), flat(cols[1], col_lane), across)
        logits = scale * logits + bias
        row = lax.broadcasted_iota(jnp.int32, logits.shape, 0)
        col = lax.broadcasted_iota(jnp.int32, logits.shape, 1)
        held = jnp.logical_and(row % ROWS < USED, col % ROWS < USED)
        return logits, held, jnp.where(held, jax.nn.sigmoid(logits), 0.0).astype(BF16)

    def own_coefficients(ref, rows, cols):
        logits, held, ref[:, own] = coefficients(rows, cols, 0)
        corner = (slice(0, ROWS), slice(0, LANES))
        logits, held = logits[corner], held[corner]
        row = lax.broadcasted_iota(jnp.int32, (ROWS, LANES), 0)
        col = lax.broadcasted_iota(jnp.int32, (ROWS, LANES), 1)
        pairs = jnp.where(row == col, -jax.nn.sigmoid(-logits), jax.nn.sigmoid(logits))
        ref[corner] = jnp.where(held, pairs, 0.0).astype(BF16)

    own, other = slice(0, half), slice(half, 2 * half)
    all_images, all_texts = (images, images_rest), (texts, texts_rest)
    own_coefficients(image_coefs, all_images, all_texts)
    own_coefficients(text_coefs, all_texts, all_images)

    def returns(coefs, cols, dz, terms, out, into, send, recv, plane):
        factor = coefs[4 * ROWS * dz : 4 * ROWS * (dz + 1), :]
        main, rest = (
            dot(factor, ref[...].reshape(2 * half, ref.shape[-1]), ((1,), (0,))).reshape(4, ROWS, ref.shape[-1])
            for ref in cols
        )
        packed = pack(main, rest)
        terms[dz] = packed[0]
        out[dz] = packed[1:4].astype(BF16)
        for k in AROUND:
            remote(out.at[dz, k - 1], into.at[dz, k - 1], send, recv.at[dz], plane[k]).start()

    def image_returns(dz):
        returns(
            image_coefs, all_texts, dz, image_terms, image_plane_out, image_plane_in, 6, image_back_recv, image_plane
        )

    def text_returns(dz):
        returns(text_coefs, all_images, dz, text_terms, text_plane_out, text_plane_in, 7, text_back_recv, text_plane)

    for dz in range(4):
        partner_complete(texts, texts_rest, text_core_recv, dz)
    image_coefs[:, other] = coefficients(all_images, all_texts, 1)[2]
    image_returns(3)
    for dz in range(4):
        partner_complete(images, images_rest, image_core_recv, dz)
    text_coefs[:, other] = coefficients(all_texts, all_images, 1)[2]
    text_returns(3)
    for dz in (2, 1):
        image_returns(dz)
        text_returns(dz)

    def summed(dz, terms, into, recv):
        arrived(into.at[dz], recv.at[dz])
        return terms[dz] + jnp.sum(into[dz].astype(F32), axis=0)

    def image_sum(dz):
        return summed(dz, image_terms, image_plane_in, image_back_recv)

    def text_sum(dz):
        return summed(dz, text_terms, text_plane_in, text_back_recv)

    def z_returns(k):
        image_z_out[k - 1] = image_sum(k).astype(BF16)
        remote(image_z_out.at[k - 1], image_z_in.at[k - 1], 8, last_recv.at[0], image_z[k]).start()
        text_z_out[k - 1] = text_sum(k).astype(BF16)
        remote(text_z_out.at[k - 1], text_z_in.at[k - 1], 9, last_recv.at[1], text_z[k]).start()

    z_returns(3)
    image_returns(0)
    text_returns(0)
    z_returns(2)
    z_returns(1)
    for blocks, first in ((texts, 0), (images, 2)):
        left(blocks.at[0, 0, pl.ds(1, 3)], first)
        left(blocks.at[0, pl.ds(1, 3)], first + 1)
        left(blocks.at[0], first // 2 + 4)
    image_total = image_sum(0)
    text_total = text_sum(0)
    left(image_plane_out, 6)
    left(text_plane_out, 7)

    def finish(i, out, total, ref):
        arrived(ref, last_recv.at[i])
        total = scale * (total + jnp.sum(ref[...].astype(F32), axis=0))
        grads[i, :, :MAIN] = total
        grads[i, :, MAIN:] = unpack_rest(total[None])[0]
        grad, unit = grads[i, 0:USED], units[i, 0:USED]
        out[...] = recip[i] * (grad - unit * jnp.sum(unit * grad, axis=1, keepdims=True))

    finish(0, image_out, image_total, image_z_in)
    finish(1, text_out, text_total, text_z_in)
    left(image_z_out, 8)
    left(text_z_out, 9)


def shards(image_embed, text_embed, logit_scale, logit_bias):
    rows, width = image_embed.shape
    vmem = pl.BlockSpec(memory_space=pltpu.VMEM)
    hbm = pl.BlockSpec(memory_space=pltpu.HBM)
    out = jax.ShapeDtypeStruct((rows, width), F32)

    def half(*lead, columns=MAIN):
        return pltpu.VMEM((*lead, ROWS, columns), BF16)

    def full(*lead, columns=MAIN):
        return pltpu.VMEM((*lead, ROWS, columns), F32)

    def dma(*shape):
        return pltpu.SemaphoreType.DMA(shape)

    return pl.pallas_call(
        kernel,
        out_shape=(out, out),
        in_specs=[pl.BlockSpec(memory_space=pltpu.SMEM)] * 2 + [hbm, hbm],
        out_specs=(vmem, vmem),
        scratch_shapes=[
            pltpu.VMEM((2, rows, width), BF16),
            full(2, columns=width),
            full(2, columns=width),
            half(2, 4, 4),
            half(2, 4, 4),
            half(2, 4, 4, columns=REST),
            half(2, 4, 4, columns=REST),
            pltpu.VMEM((16 * ROWS, 32 * ROWS), BF16),
            pltpu.VMEM((16 * ROWS, 32 * ROWS), BF16),
            full(4),
            full(4),
            half(4, 3),
            half(4, 3),
            half(4, 3),
            half(4, 3),
            half(3),
            half(3),
            half(3),
            half(3),
            dma(2),
            dma(10),
            dma(4),
            dma(4),
            dma(4),
            dma(4),
            dma(4),
            dma(4),
            dma(4),
            dma(4),
            dma(2),
        ],
        compiler_params=pltpu.CompilerParams(
            collective_id=0, has_side_effects=True, vmem_limit_bytes=40 * 1024 * 1024
        ),
    )(
        logit_scale,
        logit_bias,
        pltpu.with_memory_space_constraint(image_embed, pltpu.HBM),
        pltpu.with_memory_space_constraint(text_embed, pltpu.HBM),
    )


def solution(mesh):
    return jax.shard_map(
        shards,
        mesh=mesh,
        in_specs=(P(("blk", "grp"), None), P(("blk", "grp"), None), P(), P()),
        out_specs=(P(("blk", "grp"), None), P(("blk", "grp"), None)),
        check_vma=False,
    )
```

```python
import jax
import jax.numpy as jnp
from jax import lax
from jax.experimental import pallas as pl
from jax.experimental.pallas import tpu as pltpu
from jax.sharding import PartitionSpec as P

EPS = 1e-06
MESH = pl.DeviceIdType.MESH
ROWS = 16
USED = 12
LANES = 128
MAIN = 7 * LANES
REST = 2 * LANES
F32 = jnp.float32
BF16 = jnp.bfloat16
AROUND = (3, 2, 1)


class Place:
    def __init__(self):
        blk, grp = lax.axis_index("blk"), lax.axis_index("grp")
        self.y = blk // 2
        self.z = grp // 4
        self.x = (blk % 2) * 2 + (grp // 2) % 2
        self.core = grp % 2

    def at(self, x, y, z, core):
        return (y * 2 + x // 2, z * 4 + (x % 2) * 2 + core)

    def other_core(self):
        return self.at(self.x, self.y, self.z, 1 - self.core)

    def text_plane(self, k):
        x = self.x + (k % 2) * (1 - 2 * (self.x % 2))
        y = self.y + (k // 2) * (1 - 2 * (self.y % 2))
        return self.at(x, y, self.z, self.core)

    def image_plane(self, k):
        x = (self.x + (k % 2) * (2 * (self.x % 2) + 3)) % 4
        y = (self.y + (k // 2) * (2 * (self.y % 2) + 3)) % 4
        return self.at(x, y, self.z, self.core)

    def text_z(self, k):
        z = self.z + (k % 2) * (1 - 2 * (self.z % 2)) + (k // 2) * (4 - 8 * ((self.z // 4) % 2))
        return self.at(self.x, self.y, z, self.core)

    def image_z(self, k):
        z = self.z + (k % 2) * (2 - 4 * ((self.z // 2) % 2)) + (k // 2) * (8 * ((self.z // 4) % 2) + 12)
        return self.at(self.x, self.y, z % 16, self.core)


def pieces_up(rest):
    low, high = rest[:, 0:8], rest[:, 8:16]
    low_up, high_up = pltpu.roll(low, 4, 1), pltpu.roll(high, 4, 1)
    parts = []
    for c in (slice(0, LANES), slice(LANES, REST)):
        parts += [low_up[:, :, c], low[:, :, c], high_up[:, :, c]]
    return jnp.concatenate(parts + [jnp.zeros_like(parts[0])], axis=2)


def pack(main, rest):
    pieces = pieces_up(rest)
    lower = lax.broadcasted_iota(jnp.int32, pieces.shape, 1) >= 4
    return jnp.concatenate([main[:, 0:8], jnp.where(lower, pieces, main[:, 8:16])], axis=1)


def unpack_rest(packed):
    under = packed[:, 8:16]
    up = pltpu.roll(under, 4, 1)
    lower = lax.broadcasted_iota(jnp.int32, under[:, :, 0:LANES].shape, 1) >= 4
    lows, highs = [], []
    for c in (0, 3):
        first, second, third = (slice((c + i) * LANES, (c + i + 1) * LANES) for i in range(3))
        lows.append(jnp.where(lower, under[:, :, second], up[:, :, first]))
        highs.append(jnp.where(lower, 0.0, up[:, :, third]))
    return jnp.concatenate(
        [jnp.concatenate(lows, axis=2), jnp.concatenate(highs, axis=2)], axis=1
    )


def dot(a, b, dims):
    return lax.dot_general(a, b, (dims, ((), ())), preferred_element_type=F32)


def kernel(
    scale_ref,
    bias_ref,
    image_hbm,
    text_hbm,
    both_out,
    raw,
    units,
    grads,
    texts,
    images,
    texts_rest,
    images_rest,
    image_coefs,
    text_coefs,
    text_terms,
    image_terms,
    text_plane_out,
    text_plane_in,
    image_plane_out,
    image_plane_in,
    text_z_out,
    text_z_in,
    image_z_out,
    image_z_in,
    load_sems,
    send_sems,
    text_z_recv,
    text_plane_recv,
    image_z_recv,
    image_plane_recv,
    text_core_recv,
    image_core_recv,
    text_back_recv,
    image_back_recv,
    last_recv,
):
    loads = [
        pltpu.make_async_copy(image_hbm, raw.at[0], load_sems.at[0]),
        pltpu.make_async_copy(text_hbm, raw.at[1], load_sems.at[1]),
    ]
    for one in loads:
        one.start()
    place = Place()
    partner = place.other_core()
    text_plane, image_plane, image_z, text_z = (
        {k: way(k) for k in AROUND} for way in (place.text_plane, place.image_plane, place.image_z, place.text_z)
    )
    barrier = pltpu.get_barrier_semaphore()
    for k in AROUND:
        for device in (text_z[k], image_z[k], text_plane[k], image_plane[k]):
            pl.semaphore_signal(barrier, inc=1, device_id=device, device_id_type=MESH)
    pl.semaphore_signal(barrier, inc=1, device_id=partner, device_id_type=MESH)
    units[...] = jnp.zeros_like(units)
    for one in loads:
        one.wait()
    values = raw[...].astype(F32)
    recip = lax.rsqrt(jnp.sum(values * values, axis=2, keepdims=True) + EPS)
    units[:, 0:USED] = values * recip
    own = units[...]
    own_rest = own[:, :, MAIN:]
    own_packed = pack(own[:, :, :MAIN], own_rest).astype(BF16)
    images[0, 0, 0] = own_packed[0]
    texts[0, 0, 0] = own_packed[1]
    pl.semaphore_wait(barrier, 13)

    def remote(src, dst, send, recv, device):
        return pltpu.make_async_remote_copy(
            src_ref=src,
            dst_ref=dst,
            send_sem=send_sems.at[send],
            recv_sem=recv,
            device_id=device,
            device_id_type=MESH,
        )

    def arrived(ref, recv):
        remote(ref, ref, 0, recv, partner).wait_recv()

    def left(ref, send):
        remote(ref, ref, send, text_core_recv.at[0], partner).wait_send()

    def spread(blocks, plane, send, recv, dz):
        for k in AROUND:
            remote(blocks.at[0, dz, 0], blocks.at[0, dz, k], send, recv.at[dz], plane[k]).start()

    def to_partner(blocks, plane_recv, send, core_recv, dz):
        arrived(blocks.at[0, dz, pl.ds(1, 3)], plane_recv.at[dz])
        remote(blocks.at[0, dz], blocks.at[1, dz], send, core_recv.at[dz], partner).start()

    def unpack_set(lane, dz):
        for blocks, rests in ((texts, texts_rest), (images, images_rest)):
            rests[lane, dz] = unpack_rest(blocks[lane, dz].astype(F32)).astype(BF16)

    def partner_complete(blocks, rests, core_recv, dz):
        arrived(blocks.at[1, dz], core_recv.at[dz])
        rests[1, dz] = unpack_rest(blocks[1, dz].astype(F32)).astype(BF16)

    for k in AROUND:
        remote(texts.at[0, 0, 0], texts.at[0, k, 0], 0, text_z_recv.at[k], text_z[k]).start()
    for k in AROUND:
        remote(images.at[0, 0, 0], images.at[0, k, 0], 2, image_z_recv.at[k], image_z[k]).start()
    spread(texts, text_plane, 1, text_plane_recv, 0)
    spread(images, image_plane, 3, image_plane_recv, 0)
    def forward(dz):
        arrived(texts.at[0, dz, 0], text_z_recv.at[dz])
        spread(texts, text_plane, 1, text_plane_recv, dz)
        arrived(images.at[0, dz, 0], image_z_recv.at[dz])
        spread(images, image_plane, 3, image_plane_recv, dz)

    def across_cores(dz):
        to_partner(texts, text_plane_recv, 4, text_core_recv, dz)
        to_partner(images, image_plane_recv, 5, image_core_recv, dz)

    for dz in (1, 2, 3):
        forward(dz)
    across_cores(0)
    for dz in (1, 2, 3):
        across_cores(dz)
        unpack_set(0, dz - 1)
    unpack_set(0, 3)

    scale, bias = scale_ref[()], bias_ref[()]
    half = 16 * ROWS
    across = ((1,), (1,))

    def flat(ref, lane):
        return ref[lane].reshape(half, ref.shape[-1])

    def coefficients(rows, cols, col_lane):
        logits = dot(flat(rows[0], 0), flat(cols[0], col_lane), across)
        logits = logits + dot(flat(rows[1], 0), flat(cols[1], col_lane), across)
        logits = scale * logits + bias
        row = lax.broadcasted_iota(jnp.int32, logits.shape, 0)
        col = lax.broadcasted_iota(jnp.int32, logits.shape, 1)
        held = jnp.logical_and(row % ROWS < USED, col % ROWS < USED)
        return logits, held, jnp.where(held, jax.nn.sigmoid(logits), 0.0).astype(BF16)

    def own_coefficients(ref, rows, cols):
        logits, held, ref[:, own] = coefficients(rows, cols, 0)
        corner = (slice(0, ROWS), slice(0, LANES))
        logits, held = logits[corner], held[corner]
        row = lax.broadcasted_iota(jnp.int32, (ROWS, LANES), 0)
        col = lax.broadcasted_iota(jnp.int32, (ROWS, LANES), 1)
        pairs = jnp.where(row == col, -jax.nn.sigmoid(-logits), jax.nn.sigmoid(logits))
        ref[corner] = jnp.where(held, pairs, 0.0).astype(BF16)

    own, other = slice(0, half), slice(half, 2 * half)
    all_images, all_texts = (images, images_rest), (texts, texts_rest)
    own_coefficients(image_coefs, all_images, all_texts)
    own_coefficients(text_coefs, all_texts, all_images)

    def returns(coefs, cols, dz, terms, out, into, send, recv, plane):
        factor = coefs[4 * ROWS * dz : 4 * ROWS * (dz + 1), :]
        main, rest = (
            dot(factor, ref[...].reshape(2 * half, ref.shape[-1]), ((1,), (0,))).reshape(4, ROWS, ref.shape[-1])
            for ref in cols
        )
        packed = pack(main, rest)
        terms[dz] = packed[0]
        out[dz] = packed[1:4].astype(BF16)
        for k in AROUND:
            remote(out.at[dz, k - 1], into.at[dz, k - 1], send, recv.at[dz], plane[k]).start()

    def image_returns(dz):
        returns(
            image_coefs, all_texts, dz, image_terms, image_plane_out, image_plane_in, 6, image_back_recv, image_plane
        )

    def text_returns(dz):
        returns(text_coefs, all_images, dz, text_terms, text_plane_out, text_plane_in, 7, text_back_recv, text_plane)

    for dz in range(4):
        partner_complete(texts, texts_rest, text_core_recv, dz)
    image_coefs[:, other] = coefficients(all_images, all_texts, 1)[2]
    image_returns(3)
    for dz in range(4):
        partner_complete(images, images_rest, image_core_recv, dz)
    text_coefs[:, other] = coefficients(all_texts, all_images, 1)[2]
    text_returns(3)
    for dz in (2, 1):
        image_returns(dz)
        text_returns(dz)

    def summed(dz, terms, into, recv):
        arrived(into.at[dz], recv.at[dz])
        return terms[dz] + jnp.sum(into[dz].astype(F32), axis=0)

    def image_sum(dz):
        return summed(dz, image_terms, image_plane_in, image_back_recv)

    def text_sum(dz):
        return summed(dz, text_terms, text_plane_in, text_back_recv)

    def image_z_return(k):
        image_z_out[k - 1] = image_sum(k).astype(BF16)
        remote(image_z_out.at[k - 1], image_z_in.at[k - 1], 8, last_recv.at[0], image_z[k]).start()

    def text_z_return(k):
        text_z_out[k - 1] = text_sum(k).astype(BF16)
        remote(text_z_out.at[k - 1], text_z_in.at[k - 1], 9, last_recv.at[1], text_z[k]).start()

    image_z_return(3)
    image_returns(0)
    text_z_return(3)
    text_returns(0)
    for k in (2, 1):
        image_z_return(k)
        text_z_return(k)
    for blocks, first in ((texts, 0), (images, 2)):
        left(blocks.at[0, 0, pl.ds(1, 3)], first)
        left(blocks.at[0, pl.ds(1, 3)], first + 1)
        left(blocks.at[0], first // 2 + 4)
    image_total = image_sum(0)
    text_total = text_sum(0)
    left(image_plane_out, 6)
    left(text_plane_out, 7)

    def finish(i, total, ref):
        arrived(ref, last_recv.at[i])
        total = scale * (total + jnp.sum(ref[...].astype(F32), axis=0))
        grads[i, :, :MAIN] = total
        grads[i, :, MAIN:] = unpack_rest(total[None])[0]
        grad, unit = grads[i, 0:USED], units[i, 0:USED]
        both_out[i] = recip[i] * (grad - unit * jnp.sum(unit * grad, axis=1, keepdims=True))

    finish(0, image_total, image_z_in)
    finish(1, text_total, text_z_in)
    left(image_z_out, 8)
    left(text_z_out, 9)


def shards(image_embed, text_embed, logit_scale, logit_bias):
    rows, width = image_embed.shape
    vmem = pl.BlockSpec(memory_space=pltpu.VMEM)
    hbm = pl.BlockSpec(memory_space=pltpu.HBM)
    out = jax.ShapeDtypeStruct((rows, width), F32)

    def half(*lead, columns=MAIN):
        return pltpu.VMEM((*lead, ROWS, columns), BF16)

    def full(*lead, columns=MAIN):
        return pltpu.VMEM((*lead, ROWS, columns), F32)

    def dma(*shape):
        return pltpu.SemaphoreType.DMA(shape)

    both = pl.pallas_call(
        kernel,
        out_shape=jax.ShapeDtypeStruct((2, rows, width), F32),
        in_specs=[pl.BlockSpec(memory_space=pltpu.SMEM)] * 2 + [hbm, hbm],
        out_specs=vmem,
        scratch_shapes=[
            pltpu.VMEM((2, rows, width), BF16),
            full(2, columns=width),
            full(2, columns=width),
            half(2, 4, 4),
            half(2, 4, 4),
            half(2, 4, 4, columns=REST),
            half(2, 4, 4, columns=REST),
            pltpu.VMEM((16 * ROWS, 32 * ROWS), BF16),
            pltpu.VMEM((16 * ROWS, 32 * ROWS), BF16),
            full(4),
            full(4),
            half(4, 3),
            half(4, 3),
            half(4, 3),
            half(4, 3),
            half(3),
            half(3),
            half(3),
            half(3),
            dma(2),
            dma(10),
            dma(4),
            dma(4),
            dma(4),
            dma(4),
            dma(4),
            dma(4),
            dma(4),
            dma(4),
            dma(2),
        ],
        compiler_params=pltpu.CompilerParams(
            collective_id=0, has_side_effects=True, vmem_limit_bytes=40 * 1024 * 1024
        ),
    )(
        logit_scale,
        logit_bias,
        pltpu.with_memory_space_constraint(image_embed, pltpu.HBM),
        pltpu.with_memory_space_constraint(text_embed, pltpu.HBM),
    )
    return both[0], both[1]


def solution(mesh):
    return jax.shard_map(
        shards,
        mesh=mesh,
        in_specs=(P(("blk", "grp"), None), P(("blk", "grp"), None), P(), P()),
        out_specs=(P(("blk", "grp"), None), P(("blk", "grp"), None)),
        check_vma=False,
    )
```

```python
import jax
import jax.numpy as jnp
from jax import lax
from jax.experimental import pallas as pl
from jax.experimental.pallas import tpu as pltpu
from jax.sharding import PartitionSpec as P

EPS = 1e-06
MESH = pl.DeviceIdType.MESH
ROWS = 16
USED = 12
LANES = 128
MAIN = 7 * LANES
REST = 2 * LANES
F32 = jnp.float32
BF16 = jnp.bfloat16
AROUND = (3, 2, 1)


class Place:
    def __init__(self):
        blk, grp = lax.axis_index("blk"), lax.axis_index("grp")
        self.y = blk // 2
        self.z = grp // 4
        self.x = (blk % 2) * 2 + (grp // 2) % 2
        self.core = grp % 2

    def at(self, x, y, z, core):
        return (y * 2 + x // 2, z * 4 + (x % 2) * 2 + core)

    def other_core(self):
        return self.at(self.x, self.y, self.z, 1 - self.core)

    def text_plane(self, k):
        x = self.x + (k % 2) * (1 - 2 * (self.x % 2))
        y = self.y + (k // 2) * (1 - 2 * (self.y % 2))
        return self.at(x, y, self.z, self.core)

    def image_plane(self, k):
        x = (self.x + (k % 2) * (2 * (self.x % 2) + 3)) % 4
        y = (self.y + (k // 2) * (2 * (self.y % 2) + 3)) % 4
        return self.at(x, y, self.z, self.core)

    def text_z(self, k):
        z = self.z + (k % 2) * (1 - 2 * (self.z % 2)) + (k // 2) * (4 - 8 * ((self.z // 4) % 2))
        return self.at(self.x, self.y, z, self.core)

    def image_z(self, k):
        z = self.z + (k % 2) * (2 - 4 * ((self.z // 2) % 2)) + (k // 2) * (8 * ((self.z // 4) % 2) + 12)
        return self.at(self.x, self.y, z % 16, self.core)


def pieces_up(rest):
    low, high = rest[:, 0:8], rest[:, 8:16]
    low_up, high_up = pltpu.roll(low, 4, 1), pltpu.roll(high, 4, 1)
    parts = []
    for c in (slice(0, LANES), slice(LANES, REST)):
        parts += [low_up[:, :, c], low[:, :, c], high_up[:, :, c]]
    return jnp.concatenate(parts + [jnp.zeros_like(parts[0])], axis=2)


def pack(main, rest):
    pieces = pieces_up(rest)
    lower = lax.broadcasted_iota(jnp.int32, pieces.shape, 1) >= 4
    return jnp.concatenate([main[:, 0:8], jnp.where(lower, pieces, main[:, 8:16])], axis=1)


def unpack_rest(packed):
    under = packed[:, 8:16]
    up = pltpu.roll(under, 4, 1)
    lower = lax.broadcasted_iota(jnp.int32, under[:, :, 0:LANES].shape, 1) >= 4
    lows, highs = [], []
    for c in (0, 3):
        first, second, third = (slice((c + i) * LANES, (c + i + 1) * LANES) for i in range(3))
        lows.append(jnp.where(lower, under[:, :, second], up[:, :, first]))
        highs.append(jnp.where(lower, 0.0, up[:, :, third]))
    return jnp.concatenate(
        [jnp.concatenate(lows, axis=2), jnp.concatenate(highs, axis=2)], axis=1
    )


def dot(a, b, dims):
    return lax.dot_general(a, b, (dims, ((), ())), preferred_element_type=F32)


def kernel(
    scale_ref,
    bias_ref,
    image_hbm,
    text_hbm,
    both_out,
    raw,
    units,
    grads,
    texts,
    images,
    texts_rest,
    images_rest,
    image_coefs,
    text_coefs,
    text_terms,
    image_terms,
    text_plane_out,
    text_plane_in,
    image_plane_out,
    image_plane_in,
    text_z_out,
    text_z_in,
    image_z_out,
    image_z_in,
    load_sems,
    send_sems,
    text_z_recv,
    text_plane_recv,
    image_z_recv,
    image_plane_recv,
    text_core_recv,
    image_core_recv,
    text_back_recv,
    image_back_recv,
    last_recv,
):
    loads = [
        pltpu.make_async_copy(image_hbm, raw.at[0], load_sems.at[0]),
        pltpu.make_async_copy(text_hbm, raw.at[1], load_sems.at[1]),
    ]
    for one in loads:
        one.start()
    place = Place()
    partner = place.other_core()
    text_plane, image_plane, image_z, text_z = (
        {k: way(k) for k in AROUND} for way in (place.text_plane, place.image_plane, place.image_z, place.text_z)
    )
    barrier = pltpu.get_barrier_semaphore()
    for k in AROUND:
        for device in (text_z[k], image_z[k], text_plane[k], image_plane[k]):
            pl.semaphore_signal(barrier, inc=1, device_id=device, device_id_type=MESH)
    pl.semaphore_signal(barrier, inc=1, device_id=partner, device_id_type=MESH)
    units[...] = jnp.zeros_like(units)
    for one in loads:
        one.wait()
    values = raw[...].astype(F32)
    recip = lax.rsqrt(jnp.sum(values * values, axis=2, keepdims=True) + EPS)
    units[:, 0:USED] = values * recip
    own = units[...]
    own_rest = own[:, :, MAIN:]
    own_packed = pack(own[:, :, :MAIN], own_rest).astype(BF16)
    images[0, 0, 0] = own_packed[0]
    texts[0, 0, 0] = own_packed[1]
    pl.semaphore_wait(barrier, 13)

    def remote(src, dst, send, recv, device):
        return pltpu.make_async_remote_copy(
            src_ref=src,
            dst_ref=dst,
            send_sem=send_sems.at[send],
            recv_sem=recv,
            device_id=device,
            device_id_type=MESH,
        )

    def arrived(ref, recv):
        remote(ref, ref, 0, recv, partner).wait_recv()

    def left(ref, send):
        remote(ref, ref, send, text_core_recv.at[0], partner).wait_send()

    def spread(blocks, plane, send, recv, dz):
        for k in AROUND:
            remote(blocks.at[0, dz, 0], blocks.at[0, dz, k], send, recv.at[dz], plane[k]).start()

    def to_partner(blocks, plane_recv, send, core_recv, dz):
        arrived(blocks.at[0, dz, pl.ds(1, 3)], plane_recv.at[dz])
        remote(blocks.at[0, dz], blocks.at[1, dz], send, core_recv.at[dz], partner).start()

    def unpack_set(blocks, rests, lane, dz):
        rests[lane, dz] = unpack_rest(blocks[lane, dz].astype(F32)).astype(BF16)

    def partner_complete(blocks, rests, core_recv, dz):
        arrived(blocks.at[1, dz], core_recv.at[dz])
        unpack_set(blocks, rests, 1, dz)

    for k in AROUND:
        remote(texts.at[0, 0, 0], texts.at[0, k, 0], 0, text_z_recv.at[k], text_z[k]).start()
    for k in AROUND:
        remote(images.at[0, 0, 0], images.at[0, k, 0], 2, image_z_recv.at[k], image_z[k]).start()
    spread(texts, text_plane, 1, text_plane_recv, 0)
    spread(images, image_plane, 3, image_plane_recv, 0)
    for dz in (1, 2, 3):
        arrived(texts.at[0, dz, 0], text_z_recv.at[dz])
        spread(texts, text_plane, 1, text_plane_recv, dz)
    for dz in (1, 2, 3):
        arrived(images.at[0, dz, 0], image_z_recv.at[dz])
        spread(images, image_plane, 3, image_plane_recv, dz)
    for dz in range(4):
        to_partner(texts, text_plane_recv, 4, text_core_recv, dz)
    for dz in range(4):
        to_partner(images, image_plane_recv, 5, image_core_recv, dz)
        unpack_set(texts, texts_rest, 0, dz)
        if dz > 0:
            unpack_set(images, images_rest, 0, dz - 1)
    unpack_set(images, images_rest, 0, 3)

    scale, bias = scale_ref[()], bias_ref[()]
    half = 16 * ROWS
    across = ((1,), (1,))

    def flat(ref, lane):
        return ref[lane].reshape(half, ref.shape[-1])

    def coefficients(rows, cols, col_lane):
        logits = dot(flat(rows[0], 0), flat(cols[0], col_lane), across)
        logits = logits + dot(flat(rows[1], 0), flat(cols[1], col_lane), across)
        logits = scale * logits + bias
        row = lax.broadcasted_iota(jnp.int32, logits.shape, 0)
        col = lax.broadcasted_iota(jnp.int32, logits.shape, 1)
        held = jnp.logical_and(row % ROWS < USED, col % ROWS < USED)
        return logits, held, jnp.where(held, jax.nn.sigmoid(logits), 0.0).astype(BF16)

    def own_coefficients(ref, rows, cols):
        logits, held, ref[:, own] = coefficients(rows, cols, 0)
        corner = (slice(0, ROWS), slice(0, LANES))
        logits, held = logits[corner], held[corner]
        row = lax.broadcasted_iota(jnp.int32, (ROWS, LANES), 0)
        col = lax.broadcasted_iota(jnp.int32, (ROWS, LANES), 1)
        pairs = jnp.where(row == col, -jax.nn.sigmoid(-logits), jax.nn.sigmoid(logits))
        ref[corner] = jnp.where(held, pairs, 0.0).astype(BF16)

    own, other = slice(0, half), slice(half, 2 * half)
    all_images, all_texts = (images, images_rest), (texts, texts_rest)
    own_coefficients(image_coefs, all_images, all_texts)
    own_coefficients(text_coefs, all_texts, all_images)

    def returns(coefs, cols, dz, terms, out, into, send, recv, plane):
        factor = coefs[4 * ROWS * dz : 4 * ROWS * (dz + 1), :]
        main, rest = (
            dot(factor, ref[...].reshape(2 * half, ref.shape[-1]), ((1,), (0,))).reshape(4, ROWS, ref.shape[-1])
            for ref in cols
        )
        packed = pack(main, rest)
        terms[dz] = packed[0]
        out[dz] = packed[1:4].astype(BF16)
        for k in AROUND:
            remote(out.at[dz, k - 1], into.at[dz, k - 1], send, recv.at[dz], plane[k]).start()

    def image_returns(dz):
        returns(
            image_coefs, all_texts, dz, image_terms, image_plane_out, image_plane_in, 6, image_back_recv, image_plane
        )

    def text_returns(dz):
        returns(text_coefs, all_images, dz, text_terms, text_plane_out, text_plane_in, 7, text_back_recv, text_plane)

    for dz in range(4):
        partner_complete(texts, texts_rest, text_core_recv, dz)
    image_coefs[:, other] = coefficients(all_images, all_texts, 1)[2]
    image_returns(3)
    for dz in range(4):
        partner_complete(images, images_rest, image_core_recv, dz)
    text_coefs[:, other] = coefficients(all_texts, all_images, 1)[2]
    text_returns(3)
    for dz in (2, 1):
        image_returns(dz)
        text_returns(dz)

    def summed(dz, terms, into, recv):
        arrived(into.at[dz], recv.at[dz])
        return terms[dz] + jnp.sum(into[dz].astype(F32), axis=0)

    def image_sum(dz):
        return summed(dz, image_terms, image_plane_in, image_back_recv)

    def text_sum(dz):
        return summed(dz, text_terms, text_plane_in, text_back_recv)

    def image_z_return(k):
        image_z_out[k - 1] = image_sum(k).astype(BF16)
        remote(image_z_out.at[k - 1], image_z_in.at[k - 1], 8, last_recv.at[0], image_z[k]).start()

    def text_z_return(k):
        text_z_out[k - 1] = text_sum(k).astype(BF16)
        remote(text_z_out.at[k - 1], text_z_in.at[k - 1], 9, last_recv.at[1], text_z[k]).start()

    image_z_return(3)
    image_returns(0)
    text_z_return(3)
    text_returns(0)
    for k in (2, 1):
        image_z_return(k)
        text_z_return(k)
    for blocks, first in ((texts, 0), (images, 2)):
        left(blocks.at[0, 0, pl.ds(1, 3)], first)
        left(blocks.at[0, pl.ds(1, 3)], first + 1)
        left(blocks.at[0], first // 2 + 4)
    image_total = image_sum(0)
    text_total = text_sum(0)
    left(image_plane_out, 6)
    left(text_plane_out, 7)

    def finish(i, total, ref):
        arrived(ref, last_recv.at[i])
        total = scale * (total + jnp.sum(ref[...].astype(F32), axis=0))
        grads[i, :, :MAIN] = total
        grads[i, :, MAIN:] = unpack_rest(total[None])[0]
        grad, unit = grads[i, 0:USED], units[i, 0:USED]
        both_out[i] = recip[i] * (grad - unit * jnp.sum(unit * grad, axis=1, keepdims=True))

    finish(0, image_total, image_z_in)
    finish(1, text_total, text_z_in)
    left(image_z_out, 8)
    left(text_z_out, 9)


def shards(image_embed, text_embed, logit_scale, logit_bias):
    rows, width = image_embed.shape
    vmem = pl.BlockSpec(memory_space=pltpu.VMEM)
    hbm = pl.BlockSpec(memory_space=pltpu.HBM)
    out = jax.ShapeDtypeStruct((rows, width), F32)

    def half(*lead, columns=MAIN):
        return pltpu.VMEM((*lead, ROWS, columns), BF16)

    def full(*lead, columns=MAIN):
        return pltpu.VMEM((*lead, ROWS, columns), F32)

    def dma(*shape):
        return pltpu.SemaphoreType.DMA(shape)

    both = pl.pallas_call(
        kernel,
        out_shape=jax.ShapeDtypeStruct((2, rows, width), F32),
        in_specs=[pl.BlockSpec(memory_space=pltpu.SMEM)] * 2 + [hbm, hbm],
        out_specs=vmem,
        scratch_shapes=[
            pltpu.VMEM((2, rows, width), BF16),
            full(2, columns=width),
            full(2, columns=width),
            half(2, 4, 4),
            half(2, 4, 4),
            half(2, 4, 4, columns=REST),
            half(2, 4, 4, columns=REST),
            pltpu.VMEM((16 * ROWS, 32 * ROWS), BF16),
            pltpu.VMEM((16 * ROWS, 32 * ROWS), BF16),
            full(4),
            full(4),
            half(4, 3),
            half(4, 3),
            half(4, 3),
            half(4, 3),
            half(3),
            half(3),
            half(3),
            half(3),
            dma(2),
            dma(10),
            dma(4),
            dma(4),
            dma(4),
            dma(4),
            dma(4),
            dma(4),
            dma(4),
            dma(4),
            dma(2),
        ],
        compiler_params=pltpu.CompilerParams(
            collective_id=0, has_side_effects=True, vmem_limit_bytes=40 * 1024 * 1024
        ),
    )(
        logit_scale,
        logit_bias,
        pltpu.with_memory_space_constraint(image_embed, pltpu.HBM),
        pltpu.with_memory_space_constraint(text_embed, pltpu.HBM),
    )
    return both[0], both[1]


def solution(mesh):
    return jax.shard_map(
        shards,
        mesh=mesh,
        in_specs=(P(("blk", "grp"), None), P(("blk", "grp"), None), P(), P()),
        out_specs=(P(("blk", "grp"), None), P(("blk", "grp"), None)),
        check_vma=False,
    )
```

```python
import jax
import jax.numpy as jnp
from jax import lax
from jax.experimental import pallas as pl
from jax.experimental.pallas import tpu as pltpu
from jax.sharding import PartitionSpec as P

EPS = 1e-06
MESH = pl.DeviceIdType.MESH
ROWS = 16
USED = 12
LANES = 128
MAIN = 7 * LANES
REST = 2 * LANES
F32 = jnp.float32
BF16 = jnp.bfloat16
AROUND = (3, 2, 1)


class Place:
    def __init__(self):
        blk, grp = lax.axis_index("blk"), lax.axis_index("grp")
        self.y = blk // 2
        self.z = grp // 4
        self.x = (blk % 2) * 2 + (grp // 2) % 2
        self.core = grp % 2

    def at(self, x, y, z, core):
        return (y * 2 + x // 2, z * 4 + (x % 2) * 2 + core)

    def other_core(self):
        return self.at(self.x, self.y, self.z, 1 - self.core)

    def text_plane(self, k):
        x = self.x + (k % 2) * (1 - 2 * (self.x % 2))
        y = self.y + (k // 2) * (1 - 2 * (self.y % 2))
        return self.at(x, y, self.z, self.core)

    def image_plane(self, k):
        x = (self.x + (k % 2) * (2 * (self.x % 2) + 3)) % 4
        y = (self.y + (k // 2) * (2 * (self.y % 2) + 3)) % 4
        return self.at(x, y, self.z, self.core)

    def text_z(self, k):
        z = self.z + (k % 2) * (1 - 2 * (self.z % 2)) + (k // 2) * (4 - 8 * ((self.z // 4) % 2))
        return self.at(self.x, self.y, z, self.core)

    def image_z(self, k):
        z = self.z + (k % 2) * (2 - 4 * ((self.z // 2) % 2)) + (k // 2) * (8 * ((self.z // 4) % 2) + 12)
        return self.at(self.x, self.y, z % 16, self.core)


def pieces_up(rest):
    low, high = rest[:, 0:8], rest[:, 8:16]
    low_up, high_up = pltpu.roll(low, 4, 1), pltpu.roll(high, 4, 1)
    parts = []
    for c in (slice(0, LANES), slice(LANES, REST)):
        parts += [low_up[:, :, c], low[:, :, c], high_up[:, :, c]]
    return jnp.concatenate(parts + [jnp.zeros_like(parts[0])], axis=2)


def pack(main, rest):
    pieces = pieces_up(rest)
    lower = lax.broadcasted_iota(jnp.int32, pieces.shape, 1) >= 4
    return jnp.concatenate([main[:, 0:8], jnp.where(lower, pieces, main[:, 8:16])], axis=1)


def unpack_rest(packed):
    under = packed[:, 8:16]
    up = pltpu.roll(under, 4, 1)
    lower = lax.broadcasted_iota(jnp.int32, under[:, :, 0:LANES].shape, 1) >= 4
    lows, highs = [], []
    for c in (0, 3):
        first, second, third = (slice((c + i) * LANES, (c + i + 1) * LANES) for i in range(3))
        lows.append(jnp.where(lower, under[:, :, second], up[:, :, first]))
        highs.append(jnp.where(lower, 0.0, up[:, :, third]))
    return jnp.concatenate(
        [jnp.concatenate(lows, axis=2), jnp.concatenate(highs, axis=2)], axis=1
    )


def dot(a, b, dims):
    return lax.dot_general(a, b, (dims, ((), ())), preferred_element_type=F32)


def kernel(
    scale_ref,
    bias_ref,
    image_hbm,
    text_hbm,
    both_out,
    raw,
    units,
    grads,
    texts,
    images,
    texts_rest,
    images_rest,
    image_coefs,
    text_coefs,
    text_terms,
    image_terms,
    text_plane_out,
    text_plane_in,
    image_plane_out,
    image_plane_in,
    text_z_out,
    text_z_in,
    image_z_out,
    image_z_in,
    load_sems,
    send_sems,
    text_z_recv,
    text_plane_recv,
    image_z_recv,
    image_plane_recv,
    text_core_recv,
    image_core_recv,
    text_back_recv,
    image_back_recv,
    last_recv,
):
    loads = [
        pltpu.make_async_copy(image_hbm, raw.at[0], load_sems.at[0]),
        pltpu.make_async_copy(text_hbm, raw.at[1], load_sems.at[1]),
    ]
    for one in loads:
        one.start()
    place = Place()
    partner = place.other_core()
    text_plane, image_plane, image_z, text_z = (
        {k: way(k) for k in AROUND} for way in (place.text_plane, place.image_plane, place.image_z, place.text_z)
    )
    barrier = pltpu.get_barrier_semaphore()
    for k in AROUND:
        for device in (text_z[k], image_z[k], text_plane[k], image_plane[k]):
            pl.semaphore_signal(barrier, inc=1, device_id=device, device_id_type=MESH)
    pl.semaphore_signal(barrier, inc=1, device_id=partner, device_id_type=MESH)
    units[...] = jnp.zeros_like(units)
    for one in loads:
        one.wait()
    values = raw[...].astype(F32)
    recip = lax.rsqrt(jnp.sum(values * values, axis=2, keepdims=True) + EPS)
    units[:, 0:USED] = values * recip
    own = units[...]
    own_rest = own[:, :, MAIN:]
    own_packed = pack(own[:, :, :MAIN], own_rest).astype(BF16)
    images[0, 0, 0] = own_packed[0]
    texts[0, 0, 0] = own_packed[1]
    pl.semaphore_wait(barrier, 13)

    def remote(src, dst, send, recv, device):
        return pltpu.make_async_remote_copy(
            src_ref=src,
            dst_ref=dst,
            send_sem=send_sems.at[send],
            recv_sem=recv,
            device_id=device,
            device_id_type=MESH,
        )

    def arrived(ref, recv):
        remote(ref, ref, 0, recv, partner).wait_recv()

    def left(ref, send):
        remote(ref, ref, send, text_core_recv.at[0], partner).wait_send()

    def spread(blocks, plane, send, recv, dz):
        for k in AROUND:
            remote(blocks.at[0, dz, 0], blocks.at[0, dz, k], send, recv.at[dz], plane[k]).start()

    def to_partner(blocks, plane_recv, send, core_recv, dz):
        arrived(blocks.at[0, dz, pl.ds(1, 3)], plane_recv.at[dz])
        remote(blocks.at[0, dz], blocks.at[1, dz], send, core_recv.at[dz], partner).start()

    def unpack_set(blocks, rests, lane, dz):
        rests[lane, dz] = unpack_rest(blocks[lane, dz].astype(F32)).astype(BF16)

    def partner_complete(blocks, rests, core_recv, dz):
        arrived(blocks.at[1, dz], core_recv.at[dz])
        unpack_set(blocks, rests, 1, dz)

    for k in AROUND:
        remote(texts.at[0, 0, 0], texts.at[0, k, 0], 0, text_z_recv.at[k], text_z[k]).start()
    for k in AROUND:
        remote(images.at[0, 0, 0], images.at[0, k, 0], 2, image_z_recv.at[k], image_z[k]).start()
    spread(texts, text_plane, 1, text_plane_recv, 0)
    spread(images, image_plane, 3, image_plane_recv, 0)
    for dz in (1, 2, 3):
        arrived(texts.at[0, dz, 0], text_z_recv.at[dz])
        spread(texts, text_plane, 1, text_plane_recv, dz)
    for dz in (1, 2, 3):
        arrived(images.at[0, dz, 0], image_z_recv.at[dz])
        spread(images, image_plane, 3, image_plane_recv, dz)
    for dz in range(4):
        to_partner(texts, text_plane_recv, 4, text_core_recv, dz)
    for dz in range(4):
        to_partner(images, image_plane_recv, 5, image_core_recv, dz)
        unpack_set(texts, texts_rest, 0, dz)
        if dz > 0:
            unpack_set(images, images_rest, 0, dz - 1)
    unpack_set(images, images_rest, 0, 3)

    scale, bias = scale_ref[()], bias_ref[()]
    half = 16 * ROWS
    across = ((1,), (1,))

    def flat(ref, lane):
        return ref[lane].reshape(half, ref.shape[-1])

    def logits_of(rows, cols, col_lane):
        products = dot(flat(rows[0], 0), flat(cols[0], col_lane), across)
        products = products + dot(flat(rows[1], 0), flat(cols[1], col_lane), across)
        return scale * products + bias

    def ids(shape):
        return [lax.broadcasted_iota(jnp.int32, shape, dim) for dim in (0, 1)]

    def other_coefficients(rows, cols):
        logits = logits_of(rows, cols, 1)
        col = ids(logits.shape)[1]
        return jnp.where(col % ROWS < USED, jax.nn.sigmoid(logits), 0.0).astype(BF16)

    own, other = slice(0, half), slice(half, 2 * half)
    all_images, all_texts = (images, images_rest), (texts, texts_rest)
    logits = logits_of(all_images, all_texts, 0)
    row, col = ids(logits.shape)
    held = jnp.logical_and(row % ROWS < USED, col % ROWS < USED)
    image_coefs[:, own] = jnp.where(held, jax.nn.sigmoid(logits), 0.0).astype(BF16)
    corner = (slice(0, ROWS), slice(0, LANES))
    logits = logits[corner]
    row, col = ids(logits.shape)
    pairs = jnp.where(row == col, -jax.nn.sigmoid(-logits), jax.nn.sigmoid(logits))
    image_coefs[corner] = jnp.where(held[corner], pairs, 0.0).astype(BF16)
    text_coefs[:, own] = image_coefs[:, own].astype(F32).T.astype(BF16)

    def returns(coefs, cols, places, terms, out, into, send, recv, plane):
        first = places[-1]
        factor = coefs[4 * ROWS * first : 4 * ROWS * (first + 2), :]
        main, rest = (
            dot(factor, ref[...].reshape(2 * half, ref.shape[-1]), ((1,), (0,))).reshape(8, ROWS, ref.shape[-1])
            for ref in cols
        )
        packed = pack(main, rest)
        for dz in places:
            blocks = packed[4 * (dz - first) : 4 * (dz - first + 1)]
            terms[dz] = blocks[0]
            out[dz] = blocks[1:4].astype(BF16)
            for k in AROUND:
                remote(out.at[dz, k - 1], into.at[dz, k - 1], send, recv.at[dz], plane[k]).start()

    def image_returns(places):
        returns(
            image_coefs, all_texts, places, image_terms, image_plane_out, image_plane_in, 6, image_back_recv, image_plane
        )

    def text_returns(places):
        returns(text_coefs, all_images, places, text_terms, text_plane_out, text_plane_in, 7, text_back_recv, text_plane)

    for dz in range(4):
        partner_complete(texts, texts_rest, text_core_recv, dz)
    image_coefs[:, other] = other_coefficients(all_images, all_texts)
    image_returns((3, 2))
    for dz in range(4):
        partner_complete(images, images_rest, image_core_recv, dz)
    text_coefs[:, other] = other_coefficients(all_texts, all_images)
    text_returns((3, 2))
    image_returns((1, 0))
    text_returns((1, 0))

    def summed(dz, terms, into, recv):
        arrived(into.at[dz], recv.at[dz])
        return terms[dz] + jnp.sum(into[dz].astype(F32), axis=0)

    def image_sum(dz):
        return summed(dz, image_terms, image_plane_in, image_back_recv)

    def text_sum(dz):
        return summed(dz, text_terms, text_plane_in, text_back_recv)

    def image_z_return(k):
        image_z_out[k - 1] = image_sum(k).astype(BF16)
        remote(image_z_out.at[k - 1], image_z_in.at[k - 1], 8, last_recv.at[0], image_z[k]).start()

    def text_z_return(k):
        text_z_out[k - 1] = text_sum(k).astype(BF16)
        remote(text_z_out.at[k - 1], text_z_in.at[k - 1], 9, last_recv.at[1], text_z[k]).start()

    for k in AROUND:
        image_z_return(k)
        text_z_return(k)
    for blocks, first in ((texts, 0), (images, 2)):
        left(blocks.at[0, 0, pl.ds(1, 3)], first)
        left(blocks.at[0, pl.ds(1, 3)], first + 1)
        left(blocks.at[0], first // 2 + 4)
    image_total = image_sum(0)
    text_total = text_sum(0)
    left(image_plane_out, 6)
    left(text_plane_out, 7)

    def finish(i, total, ref):
        arrived(ref, last_recv.at[i])
        total = scale * (total + jnp.sum(ref[...].astype(F32), axis=0))
        grads[i, :, :MAIN] = total
        grads[i, :, MAIN:] = unpack_rest(total[None])[0]
        grad, unit = grads[i, 0:USED], units[i, 0:USED]
        both_out[i] = recip[i] * (grad - unit * jnp.sum(unit * grad, axis=1, keepdims=True))

    finish(0, image_total, image_z_in)
    finish(1, text_total, text_z_in)
    left(image_z_out, 8)
    left(text_z_out, 9)


def shards(image_embed, text_embed, logit_scale, logit_bias):
    rows, width = image_embed.shape
    vmem = pl.BlockSpec(memory_space=pltpu.VMEM)
    hbm = pl.BlockSpec(memory_space=pltpu.HBM)
    out = jax.ShapeDtypeStruct((rows, width), F32)

    def half(*lead, columns=MAIN):
        return pltpu.VMEM((*lead, ROWS, columns), BF16)

    def full(*lead, columns=MAIN):
        return pltpu.VMEM((*lead, ROWS, columns), F32)

    def dma(*shape):
        return pltpu.SemaphoreType.DMA(shape)

    both = pl.pallas_call(
        kernel,
        out_shape=jax.ShapeDtypeStruct((2, rows, width), F32),
        in_specs=[pl.BlockSpec(memory_space=pltpu.SMEM)] * 2 + [hbm, hbm],
        out_specs=vmem,
        scratch_shapes=[
            pltpu.VMEM((2, rows, width), BF16),
            full(2, columns=width),
            full(2, columns=width),
            half(2, 4, 4),
            half(2, 4, 4),
            half(2, 4, 4, columns=REST),
            half(2, 4, 4, columns=REST),
            pltpu.VMEM((16 * ROWS, 32 * ROWS), BF16),
            pltpu.VMEM((16 * ROWS, 32 * ROWS), BF16),
            full(4),
            full(4),
            half(4, 3),
            half(4, 3),
            half(4, 3),
            half(4, 3),
            half(3),
            half(3),
            half(3),
            half(3),
            dma(2),
            dma(10),
            dma(4),
            dma(4),
            dma(4),
            dma(4),
            dma(4),
            dma(4),
            dma(4),
            dma(4),
            dma(2),
        ],
        compiler_params=pltpu.CompilerParams(
            collective_id=0, has_side_effects=True, vmem_limit_bytes=40 * 1024 * 1024
        ),
    )(
        logit_scale,
        logit_bias,
        pltpu.with_memory_space_constraint(image_embed, pltpu.HBM),
        pltpu.with_memory_space_constraint(text_embed, pltpu.HBM),
    )
    return both[0], both[1]


def solution(mesh):
    return jax.shard_map(
        shards,
        mesh=mesh,
        in_specs=(P(("blk", "grp"), None), P(("blk", "grp"), None), P(), P()),
        out_specs=(P(("blk", "grp"), None), P(("blk", "grp"), None)),
        check_vma=False,
    )
```

```python
import jax
import jax.numpy as jnp
from jax import lax
from jax.experimental import pallas as pl
from jax.experimental.pallas import tpu as pltpu
from jax.sharding import PartitionSpec as P

EPS = 1e-06
MESH = pl.DeviceIdType.MESH
ROWS = 16
USED = 12
LANES = 128
MAIN = 7 * LANES
REST = 2 * LANES
F32 = jnp.float32
BF16 = jnp.bfloat16
AROUND = (3, 2, 1)


class Place:
    def __init__(self):
        blk, grp = lax.axis_index("blk"), lax.axis_index("grp")
        self.y = blk // 2
        self.z = grp // 4
        self.x = (blk % 2) * 2 + (grp // 2) % 2
        self.core = grp % 2

    def at(self, x, y, z, core):
        return (y * 2 + x // 2, z * 4 + (x % 2) * 2 + core)

    def other_core(self):
        return self.at(self.x, self.y, self.z, 1 - self.core)

    def text_plane(self, k):
        x = self.x + (k % 2) * (1 - 2 * (self.x % 2))
        y = self.y + (k // 2) * (1 - 2 * (self.y % 2))
        return self.at(x, y, self.z, self.core)

    def image_plane(self, k):
        x = (self.x + (k % 2) * (2 * (self.x % 2) + 3)) % 4
        y = (self.y + (k // 2) * (2 * (self.y % 2) + 3)) % 4
        return self.at(x, y, self.z, self.core)

    def text_z(self, k):
        z = self.z + (k % 2) * (1 - 2 * (self.z % 2)) + (k // 2) * (4 - 8 * ((self.z // 4) % 2))
        return self.at(self.x, self.y, z, self.core)

    def image_z(self, k):
        z = self.z + (k % 2) * (2 - 4 * ((self.z // 2) % 2)) + (k // 2) * (8 * ((self.z // 4) % 2) + 12)
        return self.at(self.x, self.y, z % 16, self.core)


def pieces_up(rest):
    low, high = rest[:, 0:8], rest[:, 8:16]
    low_up, high_up = pltpu.roll(low, 4, 1), pltpu.roll(high, 4, 1)
    parts = []
    for c in (slice(0, LANES), slice(LANES, REST)):
        parts += [low_up[:, :, c], low[:, :, c], high_up[:, :, c]]
    return jnp.concatenate(parts + [jnp.zeros_like(parts[0])], axis=2)


def pack(main, rest):
    pieces = pieces_up(rest)
    lower = lax.broadcasted_iota(jnp.int32, pieces.shape, 1) >= 4
    return jnp.concatenate([main[:, 0:8], jnp.where(lower, pieces, main[:, 8:16])], axis=1)


def unpack_rest(packed):
    under = packed[:, 8:16]
    up = pltpu.roll(under, 4, 1)
    lower = lax.broadcasted_iota(jnp.int32, under[:, :, 0:LANES].shape, 1) >= 4
    lows, highs = [], []
    for c in (0, 3):
        first, second, third = (slice((c + i) * LANES, (c + i + 1) * LANES) for i in range(3))
        lows.append(jnp.where(lower, under[:, :, second], up[:, :, first]))
        highs.append(jnp.where(lower, 0.0, up[:, :, third]))
    return jnp.concatenate(
        [jnp.concatenate(lows, axis=2), jnp.concatenate(highs, axis=2)], axis=1
    )


def dot(a, b, dims):
    return lax.dot_general(a, b, (dims, ((), ())), preferred_element_type=F32)


def kernel(
    scale_ref,
    bias_ref,
    image_hbm,
    text_hbm,
    both_out,
    raw,
    units,
    grads,
    texts,
    images,
    texts_rest,
    images_rest,
    image_coefs,
    text_coefs,
    text_terms,
    image_terms,
    text_plane_out,
    text_plane_in,
    image_plane_out,
    image_plane_in,
    text_z_out,
    text_z_in,
    image_z_out,
    image_z_in,
    load_sems,
    send_sems,
    text_z_recv,
    text_plane_recv,
    image_z_recv,
    image_plane_recv,
    text_core_recv,
    image_core_recv,
    text_back_recv,
    image_back_recv,
    last_recv,
):
    loads = [
        pltpu.make_async_copy(image_hbm, raw.at[0], load_sems.at[0]),
        pltpu.make_async_copy(text_hbm, raw.at[1], load_sems.at[1]),
    ]
    for one in loads:
        one.start()
    place = Place()
    partner = place.other_core()
    text_plane, image_plane, image_z, text_z = (
        {k: way(k) for k in AROUND} for way in (place.text_plane, place.image_plane, place.image_z, place.text_z)
    )
    barrier = pltpu.get_barrier_semaphore()
    for k in AROUND:
        for device in (text_z[k], image_z[k], text_plane[k], image_plane[k]):
            pl.semaphore_signal(barrier, inc=1, device_id=device, device_id_type=MESH)
    pl.semaphore_signal(barrier, inc=1, device_id=partner, device_id_type=MESH)
    units[...] = jnp.zeros_like(units)
    for one in loads:
        one.wait()
    values = raw[...].astype(F32)
    recip = lax.rsqrt(jnp.sum(values * values, axis=2, keepdims=True) + EPS)
    units[:, 0:USED] = values * recip
    own = units[...]
    own_rest = own[:, :, MAIN:]
    own_packed = pack(own[:, :, :MAIN], own_rest).astype(BF16)
    images[0, 0, 0] = own_packed[0]
    texts[0, 0, 0] = own_packed[1]
    pl.semaphore_wait(barrier, 13)

    def remote(src, dst, send, recv, device):
        return pltpu.make_async_remote_copy(
            src_ref=src,
            dst_ref=dst,
            send_sem=send_sems.at[send],
            recv_sem=recv,
            device_id=device,
            device_id_type=MESH,
        )

    def arrived(ref, recv):
        remote(ref, ref, 0, recv, partner).wait_recv()

    def left(ref, send):
        remote(ref, ref, send, text_core_recv.at[0], partner).wait_send()

    def spread(blocks, plane, send, recv, dz):
        for k in AROUND:
            remote(blocks.at[0, dz, 0], blocks.at[0, dz, k], send, recv.at[dz], plane[k]).start()

    def to_partner(blocks, plane_recv, send, core_recv, dz):
        arrived(blocks.at[0, dz, pl.ds(1, 3)], plane_recv.at[dz])
        remote(blocks.at[0, dz], blocks.at[1, dz], send, core_recv.at[dz], partner).start()

    def unpack_set(blocks, rests, lane, dz):
        rests[lane, dz] = unpack_rest(blocks[lane, dz].astype(F32)).astype(BF16)

    def partner_complete(blocks, rests, core_recv, dz):
        arrived(blocks.at[1, dz], core_recv.at[dz])
        unpack_set(blocks, rests, 1, dz)

    for k in AROUND:
        remote(texts.at[0, 0, 0], texts.at[0, k, 0], 0, text_z_recv.at[k], text_z[k]).start()
    for k in AROUND:
        remote(images.at[0, 0, 0], images.at[0, k, 0], 2, image_z_recv.at[k], image_z[k]).start()
    spread(texts, text_plane, 1, text_plane_recv, 0)
    spread(images, image_plane, 3, image_plane_recv, 0)
    for dz in (1, 2, 3):
        arrived(texts.at[0, dz, 0], text_z_recv.at[dz])
        spread(texts, text_plane, 1, text_plane_recv, dz)
    for dz in (1, 2, 3):
        arrived(images.at[0, dz, 0], image_z_recv.at[dz])
        spread(images, image_plane, 3, image_plane_recv, dz)
    for dz in range(4):
        to_partner(texts, text_plane_recv, 4, text_core_recv, dz)
    for dz in range(4):
        to_partner(images, image_plane_recv, 5, image_core_recv, dz)
        unpack_set(texts, texts_rest, 0, dz)
        if dz > 0:
            unpack_set(images, images_rest, 0, dz - 1)
    unpack_set(images, images_rest, 0, 3)

    scale, bias = scale_ref[()], bias_ref[()]
    half = 16 * ROWS
    across = ((1,), (1,))

    def flat(ref, lane):
        return ref[lane].reshape(half, ref.shape[-1])

    def logits_of(rows, cols, col_lane):
        products = dot(flat(rows[0], 0), flat(cols[0], col_lane), across)
        products = products + dot(flat(rows[1], 0), flat(cols[1], col_lane), across)
        return scale * products + bias

    def ids(shape):
        return [lax.broadcasted_iota(jnp.int32, shape, dim) for dim in (0, 1)]

    def other_coefficients(rows, cols):
        logits = logits_of(rows, cols, 1)
        col = ids(logits.shape)[1]
        return jnp.where(col % ROWS < USED, jax.nn.sigmoid(logits), 0.0).astype(BF16)

    own, other = slice(0, half), slice(half, 2 * half)
    all_images, all_texts = (images, images_rest), (texts, texts_rest)
    logits = logits_of(all_images, all_texts, 0)
    row, col = ids(logits.shape)
    held = jnp.logical_and(row % ROWS < USED, col % ROWS < USED)
    image_coefs[:, own] = jnp.where(held, jax.nn.sigmoid(logits), 0.0).astype(BF16)
    corner = (slice(0, ROWS), slice(0, LANES))
    logits = logits[corner]
    row, col = ids(logits.shape)
    pairs = jnp.where(row == col, -jax.nn.sigmoid(-logits), jax.nn.sigmoid(logits))
    image_coefs[corner] = jnp.where(held[corner], pairs, 0.0).astype(BF16)

    def returns(coefs, cols, places, terms, out, into, send, recv, plane):
        first = places[-1]
        factor = coefs[4 * ROWS * first : 4 * ROWS * (first + 2), :]
        main, rest = (
            dot(factor, ref[...].reshape(2 * half, ref.shape[-1]), ((1,), (0,))).reshape(8, ROWS, ref.shape[-1])
            for ref in cols
        )
        packed = pack(main, rest)
        for dz in places:
            blocks = packed[4 * (dz - first) : 4 * (dz - first + 1)]
            terms[dz] = blocks[0]
            out[dz] = blocks[1:4].astype(BF16)
            for k in AROUND:
                remote(out.at[dz, k - 1], into.at[dz, k - 1], send, recv.at[dz], plane[k]).start()

    def image_returns(places):
        returns(
            image_coefs, all_texts, places, image_terms, image_plane_out, image_plane_in, 6, image_back_recv, image_plane
        )

    def text_returns(places):
        returns(text_coefs, all_images, places, text_terms, text_plane_out, text_plane_in, 7, text_back_recv, text_plane)

    for dz in range(4):
        partner_complete(texts, texts_rest, text_core_recv, dz)
    image_coefs[:, other] = other_coefficients(all_images, all_texts)
    image_returns((3, 2))
    text_coefs[:, own] = image_coefs[:, own].astype(F32).T.astype(BF16)
    for dz in range(4):
        partner_complete(images, images_rest, image_core_recv, dz)
    text_coefs[:, other] = other_coefficients(all_texts, all_images)
    text_returns((3, 2))
    image_returns((1, 0))
    text_returns((1, 0))

    def summed(dz, terms, into, recv):
        arrived(into.at[dz], recv.at[dz])
        return terms[dz] + jnp.sum(into[dz].astype(F32), axis=0)

    def image_sum(dz):
        return summed(dz, image_terms, image_plane_in, image_back_recv)

    def text_sum(dz):
        return summed(dz, text_terms, text_plane_in, text_back_recv)

    def image_z_return(k):
        image_z_out[k - 1] = image_sum(k).astype(BF16)
        remote(image_z_out.at[k - 1], image_z_in.at[k - 1], 8, last_recv.at[0], image_z[k]).start()

    def text_z_return(k):
        text_z_out[k - 1] = text_sum(k).astype(BF16)
        remote(text_z_out.at[k - 1], text_z_in.at[k - 1], 9, last_recv.at[1], text_z[k]).start()

    image_z_return(3)
    image_z_return(2)
    text_z_return(3)
    text_z_return(2)
    image_z_return(1)
    text_z_return(1)
    for blocks, first in ((texts, 0), (images, 2)):
        left(blocks.at[0, 0, pl.ds(1, 3)], first)
        left(blocks.at[0, pl.ds(1, 3)], first + 1)
        left(blocks.at[0], first // 2 + 4)
    image_total = image_sum(0)
    text_total = text_sum(0)
    left(image_plane_out, 6)
    left(text_plane_out, 7)

    def finish(i, total, ref):
        arrived(ref, last_recv.at[i])
        total = scale * (total + jnp.sum(ref[...].astype(F32), axis=0))
        grads[i, :, :MAIN] = total
        grads[i, :, MAIN:] = unpack_rest(total[None])[0]
        grad, unit = grads[i, 0:USED], units[i, 0:USED]
        both_out[i] = recip[i] * (grad - unit * jnp.sum(unit * grad, axis=1, keepdims=True))

    finish(0, image_total, image_z_in)
    finish(1, text_total, text_z_in)
    left(image_z_out, 8)
    left(text_z_out, 9)


def shards(image_embed, text_embed, logit_scale, logit_bias):
    rows, width = image_embed.shape
    vmem = pl.BlockSpec(memory_space=pltpu.VMEM)
    hbm = pl.BlockSpec(memory_space=pltpu.HBM)
    out = jax.ShapeDtypeStruct((rows, width), F32)

    def half(*lead, columns=MAIN):
        return pltpu.VMEM((*lead, ROWS, columns), BF16)

    def full(*lead, columns=MAIN):
        return pltpu.VMEM((*lead, ROWS, columns), F32)

    def dma(*shape):
        return pltpu.SemaphoreType.DMA(shape)

    both = pl.pallas_call(
        kernel,
        out_shape=jax.ShapeDtypeStruct((2, rows, width), F32),
        in_specs=[pl.BlockSpec(memory_space=pltpu.SMEM)] * 2 + [hbm, hbm],
        out_specs=vmem,
        scratch_shapes=[
            pltpu.VMEM((2, rows, width), BF16),
            full(2, columns=width),
            full(2, columns=width),
            half(2, 4, 4),
            half(2, 4, 4),
            half(2, 4, 4, columns=REST),
            half(2, 4, 4, columns=REST),
            pltpu.VMEM((16 * ROWS, 32 * ROWS), BF16),
            pltpu.VMEM((16 * ROWS, 32 * ROWS), BF16),
            full(4),
            full(4),
            half(4, 3),
            half(4, 3),
            half(4, 3),
            half(4, 3),
            half(3),
            half(3),
            half(3),
            half(3),
            dma(2),
            dma(10),
            dma(4),
            dma(4),
            dma(4),
            dma(4),
            dma(4),
            dma(4),
            dma(4),
            dma(4),
            dma(2),
        ],
        compiler_params=pltpu.CompilerParams(
            collective_id=0, has_side_effects=True, vmem_limit_bytes=40 * 1024 * 1024
        ),
    )(
        logit_scale,
        logit_bias,
        pltpu.with_memory_space_constraint(image_embed, pltpu.HBM),
        pltpu.with_memory_space_constraint(text_embed, pltpu.HBM),
    )
    return both[0], both[1]


def solution(mesh):
    return jax.shard_map(
        shards,
        mesh=mesh,
        in_specs=(P(("blk", "grp"), None), P(("blk", "grp"), None), P(), P()),
        out_specs=(P(("blk", "grp"), None), P(("blk", "grp"), None)),
        check_vma=False,
    )
```

```python
import jax
import jax.numpy as jnp
from jax import lax
from jax.experimental import pallas as pl
from jax.experimental.pallas import tpu as pltpu
from jax.sharding import PartitionSpec as P

EPS = 1e-06
MESH = pl.DeviceIdType.MESH
ROWS = 16
USED = 12
LANES = 128
MAIN = 7 * LANES
REST = 2 * LANES
F32 = jnp.float32
BF16 = jnp.bfloat16
AROUND = (3, 2, 1)


class Place:
    def __init__(self):
        blk, grp = lax.axis_index("blk"), lax.axis_index("grp")
        self.y = blk // 2
        self.z = grp // 4
        self.x = (blk % 2) * 2 + (grp // 2) % 2
        self.core = grp % 2

    def at(self, x, y, z, core):
        return (y * 2 + x // 2, z * 4 + (x % 2) * 2 + core)

    def other_core(self):
        return self.at(self.x, self.y, self.z, 1 - self.core)

    def text_plane(self, k, lane=0):
        x = self.x + (k % 2) * (1 - 2 * (self.x % 2))
        y = self.y + (k // 2) * (1 - 2 * (self.y % 2))
        return self.at(x, y, self.z, self.core + lane * (1 - 2 * self.core))

    def image_plane(self, k, lane=0):
        x = (self.x + (k % 2) * (2 * (self.x % 2) + 3)) % 4
        y = (self.y + (k // 2) * (2 * (self.y % 2) + 3)) % 4
        return self.at(x, y, self.z, self.core + lane * (1 - 2 * self.core))

    def text_z(self, k):
        z = self.z + (k % 2) * (1 - 2 * (self.z % 2)) + (k // 2) * (4 - 8 * ((self.z // 4) % 2))
        return self.at(self.x, self.y, z, self.core)

    def image_z(self, k):
        z = self.z + (k % 2) * (2 - 4 * ((self.z // 2) % 2)) + (k // 2) * (8 * ((self.z // 4) % 2) + 12)
        return self.at(self.x, self.y, z % 16, self.core)


def pieces_up(rest):
    low, high = rest[:, 0:8], rest[:, 8:16]
    low_up, high_up = pltpu.roll(low, 4, 1), pltpu.roll(high, 4, 1)
    parts = []
    for c in (slice(0, LANES), slice(LANES, REST)):
        parts += [low_up[:, :, c], low[:, :, c], high_up[:, :, c]]
    return jnp.concatenate(parts + [jnp.zeros_like(parts[0])], axis=2)


def pack(main, rest):
    pieces = pieces_up(rest)
    lower = lax.broadcasted_iota(jnp.int32, pieces.shape, 1) >= 4
    return jnp.concatenate([main[:, 0:8], jnp.where(lower, pieces, main[:, 8:16])], axis=1)


def unpack_rest(packed):
    under = packed[:, 8:16]
    up = pltpu.roll(under, 4, 1)
    lower = lax.broadcasted_iota(jnp.int32, under[:, :, 0:LANES].shape, 1) >= 4
    lows, highs = [], []
    for c in (0, 3):
        first, second, third = (slice((c + i) * LANES, (c + i + 1) * LANES) for i in range(3))
        lows.append(jnp.where(lower, under[:, :, second], up[:, :, first]))
        highs.append(jnp.where(lower, 0.0, up[:, :, third]))
    return jnp.concatenate(
        [jnp.concatenate(lows, axis=2), jnp.concatenate(highs, axis=2)], axis=1
    )


def dot(a, b, dims):
    return lax.dot_general(a, b, (dims, ((), ())), preferred_element_type=F32)


def kernel(
    scale_ref,
    bias_ref,
    image_hbm,
    text_hbm,
    both_out,
    raw,
    units,
    grads,
    texts,
    images,
    texts_rest,
    images_rest,
    image_coefs,
    text_coefs,
    text_terms,
    image_terms,
    text_plane_out,
    text_plane_in,
    image_plane_out,
    image_plane_in,
    text_z_out,
    text_z_in,
    image_z_out,
    image_z_in,
    load_sems,
    send_sems,
    text_z_recv,
    text_plane_recv,
    image_z_recv,
    image_plane_recv,
    text_core_recv,
    image_core_recv,
    text_back_recv,
    image_back_recv,
    last_recv,
):
    loads = [
        pltpu.make_async_copy(image_hbm, raw.at[0], load_sems.at[0]),
        pltpu.make_async_copy(text_hbm, raw.at[1], load_sems.at[1]),
    ]
    for one in loads:
        one.start()
    place = Place()
    partner = place.other_core()
    text_plane, image_plane, image_z, text_z = (
        {k: way(k) for k in AROUND} for way in (place.text_plane, place.image_plane, place.image_z, place.text_z)
    )
    text_across, image_across = ({k: way(k, 1) for k in AROUND} for way in (place.text_plane, place.image_plane))
    barrier = pltpu.get_barrier_semaphore()
    for k in AROUND:
        for device in (text_z[k], image_z[k], text_plane[k], image_plane[k], text_across[k], image_across[k]):
            pl.semaphore_signal(barrier, inc=1, device_id=device, device_id_type=MESH)
    pl.semaphore_signal(barrier, inc=1, device_id=partner, device_id_type=MESH)
    units[...] = jnp.zeros_like(units)
    for one in loads:
        one.wait()
    values = raw[...].astype(F32)
    recip = lax.rsqrt(jnp.sum(values * values, axis=2, keepdims=True) + EPS)
    units[:, 0:USED] = values * recip
    own = units[...]
    own_rest = own[:, :, MAIN:]
    own_packed = pack(own[:, :, :MAIN], own_rest).astype(BF16)
    images[0, 0, 0] = own_packed[0]
    texts[0, 0, 0] = own_packed[1]
    pl.semaphore_wait(barrier, 19)

    def remote(src, dst, send, recv, device):
        return pltpu.make_async_remote_copy(
            src_ref=src,
            dst_ref=dst,
            send_sem=send_sems.at[send],
            recv_sem=recv,
            device_id=device,
            device_id_type=MESH,
        )

    def arrived(ref, recv):
        remote(ref, ref, 0, recv, partner).wait_recv()

    def left(ref, send):
        remote(ref, ref, send, text_core_recv.at[0], partner).wait_send()

    def spread(blocks, plane, send, recv, dz):
        for k in AROUND:
            remote(blocks.at[0, dz, 0], blocks.at[0, dz, k], send, recv.at[dz], plane[k]).start()

    def to_partner(blocks, plane_recv, send, core_recv, dz):
        arrived(blocks.at[0, dz, pl.ds(1, 3)], plane_recv.at[dz])
        if dz > 0:
            remote(blocks.at[0, dz], blocks.at[1, dz], send, core_recv.at[dz], partner).start()

    def unpack_set(blocks, rests, lane, dz):
        rests[lane, dz] = unpack_rest(blocks[lane, dz].astype(F32)).astype(BF16)

    def partner_complete(blocks, rests, core_recv, dz):
        arrived(blocks.at[1, dz], core_recv.at[dz])
        unpack_set(blocks, rests, 1, dz)

    for k in AROUND:
        remote(texts.at[0, 0, 0], texts.at[0, k, 0], 0, text_z_recv.at[k], text_z[k]).start()
    for k in AROUND:
        remote(images.at[0, 0, 0], images.at[0, k, 0], 2, image_z_recv.at[k], image_z[k]).start()
    spread(texts, text_plane, 1, text_plane_recv, 0)
    spread(images, image_plane, 3, image_plane_recv, 0)

    for i, (blocks, across_plane, recv) in enumerate(
        ((texts, text_across, text_core_recv), (images, image_across, image_core_recv))
    ):
        for k in AROUND:
            remote(blocks.at[0, 0, 0], blocks.at[1, 0, k], 10 + i, recv.at[0], across_plane[k]).start()
        remote(blocks.at[0, 0, 0], blocks.at[1, 0, 0], 12 + i, recv.at[0], partner).start()
    for dz in (1, 2, 3):
        arrived(texts.at[0, dz, 0], text_z_recv.at[dz])
        spread(texts, text_plane, 1, text_plane_recv, dz)
    for dz in (1, 2, 3):
        arrived(images.at[0, dz, 0], image_z_recv.at[dz])
        spread(images, image_plane, 3, image_plane_recv, dz)
    for dz in range(4):
        to_partner(texts, text_plane_recv, 4, text_core_recv, dz)
    for dz in range(4):
        to_partner(images, image_plane_recv, 5, image_core_recv, dz)
        unpack_set(texts, texts_rest, 0, dz)
        if dz > 0:
            unpack_set(images, images_rest, 0, dz - 1)
    unpack_set(images, images_rest, 0, 3)

    scale, bias = scale_ref[()], bias_ref[()]
    half = 16 * ROWS
    across = ((1,), (1,))

    def flat(ref, lane):
        return ref[lane].reshape(half, ref.shape[-1])

    def logits_of(rows, cols, col_lane):
        products = dot(flat(rows[0], 0), flat(cols[0], col_lane), across)
        products = products + dot(flat(rows[1], 0), flat(cols[1], col_lane), across)
        return scale * products + bias

    def ids(shape):
        return [lax.broadcasted_iota(jnp.int32, shape, dim) for dim in (0, 1)]

    def other_coefficients(rows, cols):
        logits = logits_of(rows, cols, 1)
        col = ids(logits.shape)[1]
        return jnp.where(col % ROWS < USED, jax.nn.sigmoid(logits), 0.0).astype(BF16)

    own, other = slice(0, half), slice(half, 2 * half)
    all_images, all_texts = (images, images_rest), (texts, texts_rest)
    logits = logits_of(all_images, all_texts, 0)
    row, col = ids(logits.shape)
    held = jnp.logical_and(row % ROWS < USED, col % ROWS < USED)
    image_coefs[:, own] = jnp.where(held, jax.nn.sigmoid(logits), 0.0).astype(BF16)
    corner = (slice(0, ROWS), slice(0, LANES))
    logits = logits[corner]
    row, col = ids(logits.shape)
    pairs = jnp.where(row == col, -jax.nn.sigmoid(-logits), jax.nn.sigmoid(logits))
    image_coefs[corner] = jnp.where(held[corner], pairs, 0.0).astype(BF16)

    def returns(coefs, cols, places, terms, out, into, send, recv, plane):
        first = places[-1]
        factor = coefs[4 * ROWS * first : 4 * ROWS * (first + 2), :]
        main, rest = (
            dot(factor, ref[...].reshape(2 * half, ref.shape[-1]), ((1,), (0,))).reshape(8, ROWS, ref.shape[-1])
            for ref in cols
        )
        packed = pack(main, rest)
        for dz in places:
            blocks = packed[4 * (dz - first) : 4 * (dz - first + 1)]
            terms[dz] = blocks[0]
            out[dz] = blocks[1:4].astype(BF16)
            for k in AROUND:
                remote(out.at[dz, k - 1], into.at[dz, k - 1], send, recv.at[dz], plane[k]).start()

    def image_returns(places):
        returns(
            image_coefs, all_texts, places, image_terms, image_plane_out, image_plane_in, 6, image_back_recv, image_plane
        )

    def text_returns(places):
        returns(text_coefs, all_images, places, text_terms, text_plane_out, text_plane_in, 7, text_back_recv, text_plane)

    for dz in range(4):
        partner_complete(texts, texts_rest, text_core_recv, dz)
    image_coefs[:, other] = other_coefficients(all_images, all_texts)
    image_returns((3, 2))
    text_coefs[:, own] = image_coefs[:, own].astype(F32).T.astype(BF16)
    for dz in range(4):
        partner_complete(images, images_rest, image_core_recv, dz)
    text_coefs[:, other] = other_coefficients(all_texts, all_images)
    text_returns((3, 2))
    image_returns((1, 0))
    text_returns((1, 0))

    def summed(dz, terms, into, recv):
        arrived(into.at[dz], recv.at[dz])
        return terms[dz] + jnp.sum(into[dz].astype(F32), axis=0)

    def image_sum(dz):
        return summed(dz, image_terms, image_plane_in, image_back_recv)

    def text_sum(dz):
        return summed(dz, text_terms, text_plane_in, text_back_recv)

    def image_z_return(k):
        image_z_out[k - 1] = image_sum(k).astype(BF16)
        remote(image_z_out.at[k - 1], image_z_in.at[k - 1], 8, last_recv.at[0], image_z[k]).start()

    def text_z_return(k):
        text_z_out[k - 1] = text_sum(k).astype(BF16)
        remote(text_z_out.at[k - 1], text_z_in.at[k - 1], 9, last_recv.at[1], text_z[k]).start()

    image_z_return(3)
    image_z_return(2)
    text_z_return(3)
    text_z_return(2)
    image_z_return(1)
    text_z_return(1)
    for blocks, first in ((texts, 0), (images, 2)):
        left(blocks.at[0, 0, pl.ds(1, 3)], first)
        left(blocks.at[0, pl.ds(1, 3)], first + 1)
        left(blocks.at[0, pl.ds(1, 3)], first // 2 + 4)
        left(blocks.at[0, 0, pl.ds(1, 3)], first // 2 + 10)
        left(blocks.at[0, 0, 0], first // 2 + 12)
    image_total = image_sum(0)
    text_total = text_sum(0)
    left(image_plane_out, 6)
    left(text_plane_out, 7)

    def finish(i, total, ref):
        arrived(ref, last_recv.at[i])
        total = scale * (total + jnp.sum(ref[...].astype(F32), axis=0))
        grads[i, :, :MAIN] = total
        grads[i, :, MAIN:] = unpack_rest(total[None])[0]
        grad, unit = grads[i, 0:USED], units[i, 0:USED]
        both_out[i] = recip[i] * (grad - unit * jnp.sum(unit * grad, axis=1, keepdims=True))

    finish(0, image_total, image_z_in)
    finish(1, text_total, text_z_in)
    left(image_z_out, 8)
    left(text_z_out, 9)


def shards(image_embed, text_embed, logit_scale, logit_bias):
    rows, width = image_embed.shape
    vmem = pl.BlockSpec(memory_space=pltpu.VMEM)
    hbm = pl.BlockSpec(memory_space=pltpu.HBM)
    out = jax.ShapeDtypeStruct((rows, width), F32)

    def half(*lead, columns=MAIN):
        return pltpu.VMEM((*lead, ROWS, columns), BF16)

    def full(*lead, columns=MAIN):
        return pltpu.VMEM((*lead, ROWS, columns), F32)

    def dma(*shape):
        return pltpu.SemaphoreType.DMA(shape)

    both = pl.pallas_call(
        kernel,
        out_shape=jax.ShapeDtypeStruct((2, rows, width), F32),
        in_specs=[pl.BlockSpec(memory_space=pltpu.SMEM)] * 2 + [hbm, hbm],
        out_specs=vmem,
        scratch_shapes=[
            pltpu.VMEM((2, rows, width), BF16),
            full(2, columns=width),
            full(2, columns=width),
            half(2, 4, 4),
            half(2, 4, 4),
            half(2, 4, 4, columns=REST),
            half(2, 4, 4, columns=REST),
            pltpu.VMEM((16 * ROWS, 32 * ROWS), BF16),
            pltpu.VMEM((16 * ROWS, 32 * ROWS), BF16),
            full(4),
            full(4),
            half(4, 3),
            half(4, 3),
            half(4, 3),
            half(4, 3),
            half(3),
            half(3),
            half(3),
            half(3),
            dma(2),
            dma(14),
            dma(4),
            dma(4),
            dma(4),
            dma(4),
            dma(4),
            dma(4),
            dma(4),
            dma(4),
            dma(2),
        ],
        compiler_params=pltpu.CompilerParams(
            collective_id=0, has_side_effects=True, vmem_limit_bytes=40 * 1024 * 1024
        ),
    )(
        logit_scale,
        logit_bias,
        pltpu.with_memory_space_constraint(image_embed, pltpu.HBM),
        pltpu.with_memory_space_constraint(text_embed, pltpu.HBM),
    )
    return both[0], both[1]


def solution(mesh):
    return jax.shard_map(
        shards,
        mesh=mesh,
        in_specs=(P(("blk", "grp"), None), P(("blk", "grp"), None), P(), P()),
        out_specs=(P(("blk", "grp"), None), P(("blk", "grp"), None)),
        check_vma=False,
    )
```

```python
import jax
import jax.numpy as jnp
from jax import lax
from jax.experimental import pallas as pl
from jax.experimental.pallas import tpu as pltpu
from jax.sharding import PartitionSpec as P

EPS = 1e-06
MESH = pl.DeviceIdType.MESH
ROWS = 16
USED = 12
LANES = 128
MAIN = 7 * LANES
REST = 2 * LANES
F32 = jnp.float32
BF16 = jnp.bfloat16
AROUND = (3, 2, 1)


class Place:
    def __init__(self):
        blk, grp = lax.axis_index("blk"), lax.axis_index("grp")
        self.y = blk // 2
        self.z = grp // 4
        self.x = (blk % 2) * 2 + (grp // 2) % 2
        self.core = grp % 2

    def at(self, x, y, z, core):
        return (y * 2 + x // 2, z * 4 + (x % 2) * 2 + core)

    def other_core(self):
        return self.at(self.x, self.y, self.z, 1 - self.core)

    def text_plane(self, k):
        x = self.x + (k % 2) * (1 - 2 * (self.x % 2))
        y = self.y + (k // 2) * (1 - 2 * (self.y % 2))
        return self.at(x, y, self.z, self.core)

    def image_plane(self, k):
        x = (self.x + (k % 2) * (2 * (self.x % 2) + 3)) % 4
        y = (self.y + (k // 2) * (2 * (self.y % 2) + 3)) % 4
        return self.at(x, y, self.z, self.core)

    def text_z(self, k):
        z = self.z + (k % 2) * (1 - 2 * (self.z % 2)) + (k // 2) * (4 - 8 * ((self.z // 4) % 2))
        return self.at(self.x, self.y, z, self.core)

    def image_z(self, k):
        z = self.z + (k % 2) * (2 - 4 * ((self.z // 2) % 2)) + (k // 2) * (8 * ((self.z // 4) % 2) + 12)
        return self.at(self.x, self.y, z % 16, self.core)


def pieces_up(rest):
    low, high = rest[:, 0:8], rest[:, 8:16]
    low_up, high_up = pltpu.roll(low, 4, 1), pltpu.roll(high, 4, 1)
    parts = []
    for c in (slice(0, LANES), slice(LANES, REST)):
        parts += [low_up[:, :, c], low[:, :, c], high_up[:, :, c]]
    return jnp.concatenate(parts + [jnp.zeros_like(parts[0])], axis=2)


def pack(main, rest):
    pieces = pieces_up(rest)
    lower = lax.broadcasted_iota(jnp.int32, pieces.shape, 1) >= 4
    return jnp.concatenate([main[:, 0:8], jnp.where(lower, pieces, main[:, 8:16])], axis=1)


def unpack_rest(packed):
    under = packed[:, 8:16]
    up = pltpu.roll(under, 4, 1)
    lower = lax.broadcasted_iota(jnp.int32, under[:, :, 0:LANES].shape, 1) >= 4
    lows, highs = [], []
    for c in (0, 3):
        first, second, third = (slice((c + i) * LANES, (c + i + 1) * LANES) for i in range(3))
        lows.append(jnp.where(lower, under[:, :, second], up[:, :, first]))
        highs.append(jnp.where(lower, 0.0, up[:, :, third]))
    return jnp.concatenate(
        [jnp.concatenate(lows, axis=2), jnp.concatenate(highs, axis=2)], axis=1
    )


def dot(a, b, dims):
    return lax.dot_general(a, b, (dims, ((), ())), preferred_element_type=F32)


def kernel(
    scale_ref,
    bias_ref,
    image_hbm,
    text_hbm,
    both_out,
    raw,
    units,
    grads,
    texts,
    images,
    texts_rest,
    images_rest,
    image_coefs,
    text_coefs,
    text_terms,
    image_terms,
    text_plane_out,
    text_plane_in,
    image_plane_out,
    image_plane_in,
    text_z_out,
    text_z_in,
    image_z_out,
    image_z_in,
    load_sems,
    send_sems,
    text_z_recv,
    text_plane_recv,
    image_z_recv,
    image_plane_recv,
    text_core_recv,
    image_core_recv,
    text_back_recv,
    image_back_recv,
    last_recv,
):
    loads = [
        pltpu.make_async_copy(image_hbm, raw.at[0], load_sems.at[0]),
        pltpu.make_async_copy(text_hbm, raw.at[1], load_sems.at[1]),
    ]
    for one in loads:
        one.start()
    place = Place()
    partner = place.other_core()
    text_plane, image_plane, image_z, text_z = (
        {k: way(k) for k in AROUND} for way in (place.text_plane, place.image_plane, place.image_z, place.text_z)
    )
    barrier = pltpu.get_barrier_semaphore()
    for k in AROUND:
        for device in (text_z[k], image_z[k], text_plane[k], image_plane[k]):
            pl.semaphore_signal(barrier, inc=1, device_id=device, device_id_type=MESH)
    pl.semaphore_signal(barrier, inc=1, device_id=partner, device_id_type=MESH)
    units[...] = jnp.zeros_like(units)
    for one in loads:
        one.wait()
    values = raw[...].astype(F32)
    recip = lax.rsqrt(jnp.sum(values * values, axis=2, keepdims=True) + EPS)
    units[:, 0:USED] = values * recip
    own = units[...]
    own_rest = own[:, :, MAIN:]
    own_packed = pack(own[:, :, :MAIN], own_rest).astype(BF16)
    images[0, 0, 0] = own_packed[0]
    texts[0, 0, 0] = own_packed[1]
    pl.semaphore_wait(barrier, 13)

    def remote(src, dst, send, recv, device):
        return pltpu.make_async_remote_copy(
            src_ref=src,
            dst_ref=dst,
            send_sem=send_sems.at[send],
            recv_sem=recv,
            device_id=device,
            device_id_type=MESH,
        )

    def arrived(ref, recv):
        remote(ref, ref, 0, recv, partner).wait_recv()

    def left(ref, send):
        remote(ref, ref, send, text_core_recv.at[0], partner).wait_send()

    def spread(blocks, plane, send, recv, dz):
        for k in AROUND:
            remote(blocks.at[0, dz, 0], blocks.at[0, dz, k], send, recv.at[dz], plane[k]).start()

    def to_partner(blocks, plane_recv, send, core_recv, dz):
        arrived(blocks.at[0, dz, pl.ds(1, 3)], plane_recv.at[dz])
        remote(blocks.at[0, dz], blocks.at[1, dz], send, core_recv.at[dz], partner).start()

    def unpack_set(blocks, rests, lane, dz):
        rests[lane, dz] = unpack_rest(blocks[lane, dz].astype(F32)).astype(BF16)

    def partner_complete(blocks, rests, core_recv, dz):
        arrived(blocks.at[1, dz], core_recv.at[dz])
        unpack_set(blocks, rests, 1, dz)

    for k in (1, 2, 3):
        remote(texts.at[0, 0, 0], texts.at[0, k, 0], 0, text_z_recv.at[k], text_z[k]).start()
    for k in (1, 2, 3):
        remote(images.at[0, 0, 0], images.at[0, k, 0], 2, image_z_recv.at[k], image_z[k]).start()
    spread(texts, text_plane, 1, text_plane_recv, 0)
    spread(images, image_plane, 3, image_plane_recv, 0)
    for dz in (1, 2, 3):
        arrived(texts.at[0, dz, 0], text_z_recv.at[dz])
        spread(texts, text_plane, 1, text_plane_recv, dz)
    for dz in (1, 2, 3):
        arrived(images.at[0, dz, 0], image_z_recv.at[dz])
        spread(images, image_plane, 3, image_plane_recv, dz)
    for dz in range(4):
        to_partner(texts, text_plane_recv, 4, text_core_recv, dz)
    for dz in range(4):
        to_partner(images, image_plane_recv, 5, image_core_recv, dz)
        unpack_set(texts, texts_rest, 0, dz)
        if dz > 0:
            unpack_set(images, images_rest, 0, dz - 1)
    unpack_set(images, images_rest, 0, 3)

    scale, bias = scale_ref[()], bias_ref[()]
    half = 16 * ROWS
    across = ((1,), (1,))

    def flat(ref, lane):
        return ref[lane].reshape(half, ref.shape[-1])

    def logits_of(rows, cols, col_lane):
        products = dot(flat(rows[0], 0), flat(cols[0], col_lane), across)
        products = products + dot(flat(rows[1], 0), flat(cols[1], col_lane), across)
        return scale * products + bias

    def ids(shape):
        return [lax.broadcasted_iota(jnp.int32, shape, dim) for dim in (0, 1)]

    def other_coefficients(rows, cols):
        logits = logits_of(rows, cols, 1)
        col = ids(logits.shape)[1]
        return jnp.where(col % ROWS < USED, jax.nn.sigmoid(logits), 0.0).astype(BF16)

    own, other = slice(0, half), slice(half, 2 * half)
    all_images, all_texts = (images, images_rest), (texts, texts_rest)
    logits = logits_of(all_images, all_texts, 0)
    row, col = ids(logits.shape)
    held = jnp.logical_and(row % ROWS < USED, col % ROWS < USED)
    image_coefs[:, own] = jnp.where(held, jax.nn.sigmoid(logits), 0.0).astype(BF16)
    corner = (slice(0, ROWS), slice(0, LANES))
    logits = logits[corner]
    row, col = ids(logits.shape)
    pairs = jnp.where(row == col, -jax.nn.sigmoid(-logits), jax.nn.sigmoid(logits))
    image_coefs[corner] = jnp.where(held[corner], pairs, 0.0).astype(BF16)
    text_coefs[:, own] = image_coefs[:, own].astype(F32).T.astype(BF16)

    def returns(coefs, cols, places, terms, out, into, send, recv, plane):
        first = places[-1]
        factor = coefs[4 * ROWS * first : 4 * ROWS * (first + 2), :]
        main, rest = (
            dot(factor, ref[...].reshape(2 * half, ref.shape[-1]), ((1,), (0,))).reshape(8, ROWS, ref.shape[-1])
            for ref in cols
        )
        packed = pack(main, rest)
        for dz in places:
            blocks = packed[4 * (dz - first) : 4 * (dz - first + 1)]
            terms[dz] = blocks[0]
            out[dz] = blocks[1:4].astype(BF16)
            for k in AROUND:
                remote(out.at[dz, k - 1], into.at[dz, k - 1], send, recv.at[dz], plane[k]).start()

    def image_returns(places):
        returns(
            image_coefs, all_texts, places, image_terms, image_plane_out, image_plane_in, 6, image_back_recv, image_plane
        )

    def text_returns(places):
        returns(text_coefs, all_images, places, text_terms, text_plane_out, text_plane_in, 7, text_back_recv, text_plane)

    for dz in range(4):
        partner_complete(texts, texts_rest, text_core_recv, dz)
    image_coefs[:, other] = other_coefficients(all_images, all_texts)
    image_returns((3, 2))
    for dz in range(4):
        partner_complete(images, images_rest, image_core_recv, dz)
    text_coefs[:, other] = other_coefficients(all_texts, all_images)
    text_returns((3, 2))
    image_returns((1, 0))
    text_returns((1, 0))

    def summed(dz, terms, into, recv):
        arrived(into.at[dz], recv.at[dz])
        return terms[dz] + jnp.sum(into[dz].astype(F32), axis=0)

    def image_sum(dz):
        return summed(dz, image_terms, image_plane_in, image_back_recv)

    def text_sum(dz):
        return summed(dz, text_terms, text_plane_in, text_back_recv)

    def image_z_return(k):
        image_z_out[k - 1] = image_sum(k).astype(BF16)
        remote(image_z_out.at[k - 1], image_z_in.at[k - 1], 8, last_recv.at[0], image_z[k]).start()

    def text_z_return(k):
        text_z_out[k - 1] = text_sum(k).astype(BF16)
        remote(text_z_out.at[k - 1], text_z_in.at[k - 1], 9, last_recv.at[1], text_z[k]).start()

    for k in AROUND:
        image_z_return(k)
        text_z_return(k)
    for blocks, first in ((texts, 0), (images, 2)):
        left(blocks.at[0, 0, pl.ds(1, 3)], first)
        left(blocks.at[0, pl.ds(1, 3)], first + 1)
        left(blocks.at[0], first // 2 + 4)
    image_total = image_sum(0)
    text_total = text_sum(0)
    left(image_plane_out, 6)
    left(text_plane_out, 7)

    def finish(i, total, ref):
        arrived(ref, last_recv.at[i])
        total = scale * (total + jnp.sum(ref[...].astype(F32), axis=0))
        grads[i, :, :MAIN] = total
        grads[i, :, MAIN:] = unpack_rest(total[None])[0]
        grad, unit = grads[i, 0:USED], units[i, 0:USED]
        both_out[i] = recip[i] * (grad - unit * jnp.sum(unit * grad, axis=1, keepdims=True))

    finish(0, image_total, image_z_in)
    finish(1, text_total, text_z_in)
    left(image_z_out, 8)
    left(text_z_out, 9)


def shards(image_embed, text_embed, logit_scale, logit_bias):
    rows, width = image_embed.shape
    vmem = pl.BlockSpec(memory_space=pltpu.VMEM)
    hbm = pl.BlockSpec(memory_space=pltpu.HBM)
    out = jax.ShapeDtypeStruct((rows, width), F32)

    def half(*lead, columns=MAIN):
        return pltpu.VMEM((*lead, ROWS, columns), BF16)

    def full(*lead, columns=MAIN):
        return pltpu.VMEM((*lead, ROWS, columns), F32)

    def dma(*shape):
        return pltpu.SemaphoreType.DMA(shape)

    both = pl.pallas_call(
        kernel,
        out_shape=jax.ShapeDtypeStruct((2, rows, width), F32),
        in_specs=[pl.BlockSpec(memory_space=pltpu.SMEM)] * 2 + [hbm, hbm],
        out_specs=vmem,
        scratch_shapes=[
            pltpu.VMEM((2, rows, width), BF16),
            full(2, columns=width),
            full(2, columns=width),
            half(2, 4, 4),
            half(2, 4, 4),
            half(2, 4, 4, columns=REST),
            half(2, 4, 4, columns=REST),
            pltpu.VMEM((16 * ROWS, 32 * ROWS), BF16),
            pltpu.VMEM((16 * ROWS, 32 * ROWS), BF16),
            full(4),
            full(4),
            half(4, 3),
            half(4, 3),
            half(4, 3),
            half(4, 3),
            half(3),
            half(3),
            half(3),
            half(3),
            dma(2),
            dma(10),
            dma(4),
            dma(4),
            dma(4),
            dma(4),
            dma(4),
            dma(4),
            dma(4),
            dma(4),
            dma(2),
        ],
        compiler_params=pltpu.CompilerParams(
            collective_id=0, has_side_effects=True, vmem_limit_bytes=40 * 1024 * 1024
        ),
    )(
        logit_scale,
        logit_bias,
        pltpu.with_memory_space_constraint(image_embed, pltpu.HBM),
        pltpu.with_memory_space_constraint(text_embed, pltpu.HBM),
    )
    return both[0], both[1]


def solution(mesh):
    return jax.shard_map(
        shards,
        mesh=mesh,
        in_specs=(P(("blk", "grp"), None), P(("blk", "grp"), None), P(), P()),
        out_specs=(P(("blk", "grp"), None), P(("blk", "grp"), None)),
        check_vma=False,
    )
```

```python
import jax
import jax.numpy as jnp
from jax import lax
from jax.experimental import pallas as pl
from jax.experimental.pallas import tpu as pltpu
from jax.sharding import PartitionSpec as P

EPS = 1e-06
MESH = pl.DeviceIdType.MESH
ROWS = 16
USED = 12
LANES = 128
MAIN = 7 * LANES
REST = 2 * LANES
F32 = jnp.float32
BF16 = jnp.bfloat16
AROUND = (3, 2, 1)


class Place:
    def __init__(self):
        blk, grp = lax.axis_index("blk"), lax.axis_index("grp")
        self.y = blk // 2
        self.z = grp // 4
        self.x = (blk % 2) * 2 + (grp // 2) % 2
        self.core = grp % 2

    def at(self, x, y, z, core):
        return (y * 2 + x // 2, z * 4 + (x % 2) * 2 + core)

    def other_core(self):
        return self.at(self.x, self.y, self.z, 1 - self.core)

    def text_plane(self, k):
        x = self.x + (k % 2) * (1 - 2 * (self.x % 2))
        y = self.y + (k // 2) * (1 - 2 * (self.y % 2))
        return self.at(x, y, self.z, self.core)

    def image_plane(self, k):
        x = (self.x + (k % 2) * (2 * (self.x % 2) + 3)) % 4
        y = (self.y + (k // 2) * (2 * (self.y % 2) + 3)) % 4
        return self.at(x, y, self.z, self.core)

    def text_z(self, k):
        z = self.z + (k % 2) * (1 - 2 * (self.z % 2)) + (k // 2) * (4 - 8 * ((self.z // 4) % 2))
        return self.at(self.x, self.y, z, self.core)

    def image_z(self, k):
        z = self.z + (k % 2) * (2 - 4 * ((self.z // 2) % 2)) + (k // 2) * (8 * ((self.z // 4) % 2) + 12)
        return self.at(self.x, self.y, z % 16, self.core)


def pieces_up(rest):
    low, high = rest[:, 0:8], rest[:, 8:16]
    low_up, high_up = pltpu.roll(low, 4, 1), pltpu.roll(high, 4, 1)
    parts = []
    for c in (slice(0, LANES), slice(LANES, REST)):
        parts += [low_up[:, :, c], low[:, :, c], high_up[:, :, c]]
    return jnp.concatenate(parts + [jnp.zeros_like(parts[0])], axis=2)


def pack(main, rest):
    pieces = pieces_up(rest)
    lower = lax.broadcasted_iota(jnp.int32, pieces.shape, 1) >= 4
    return jnp.concatenate([main[:, 0:8], jnp.where(lower, pieces, main[:, 8:16])], axis=1)


def unpack_rest(packed):
    under = packed[:, 8:16]
    up = pltpu.roll(under, 4, 1)
    lower = lax.broadcasted_iota(jnp.int32, under[:, :, 0:LANES].shape, 1) >= 4
    lows, highs = [], []
    for c in (0, 3):
        first, second, third = (slice((c + i) * LANES, (c + i + 1) * LANES) for i in range(3))
        lows.append(jnp.where(lower, under[:, :, second], up[:, :, first]))
        highs.append(jnp.where(lower, 0.0, up[:, :, third]))
    return jnp.concatenate(
        [jnp.concatenate(lows, axis=2), jnp.concatenate(highs, axis=2)], axis=1
    )


def dot(a, b, dims):
    return lax.dot_general(a, b, (dims, ((), ())), preferred_element_type=F32)


def kernel(
    scale_ref,
    bias_ref,
    image_hbm,
    text_hbm,
    both_out,
    raw,
    units,
    grads,
    texts,
    images,
    texts_rest,
    images_rest,
    image_coefs,
    text_coefs,
    text_terms,
    image_terms,
    text_plane_out,
    text_plane_in,
    image_plane_out,
    image_plane_in,
    text_z_out,
    text_z_in,
    image_z_out,
    image_z_in,
    load_sems,
    send_sems,
    text_z_recv,
    text_plane_recv,
    image_z_recv,
    image_plane_recv,
    text_core_recv,
    image_core_recv,
    text_back_recv,
    image_back_recv,
    last_recv,
):
    loads = [
        pltpu.make_async_copy(image_hbm, raw.at[0], load_sems.at[0]),
        pltpu.make_async_copy(text_hbm, raw.at[1], load_sems.at[1]),
    ]
    for one in loads:
        one.start()
    place = Place()
    partner = place.other_core()
    text_plane, image_plane, image_z, text_z = (
        {k: way(k) for k in AROUND} for way in (place.text_plane, place.image_plane, place.image_z, place.text_z)
    )
    barrier = pltpu.get_barrier_semaphore()
    for k in AROUND:
        for device in (text_z[k], image_z[k], text_plane[k], image_plane[k]):
            pl.semaphore_signal(barrier, inc=1, device_id=device, device_id_type=MESH)
    pl.semaphore_signal(barrier, inc=1, device_id=partner, device_id_type=MESH)
    units[...] = jnp.zeros_like(units)
    for one in loads:
        one.wait()
    values = raw[...].astype(F32)
    recip = lax.rsqrt(jnp.sum(values * values, axis=2, keepdims=True) + EPS)
    units[:, 0:USED] = values * recip
    own = units[...]
    own_rest = own[:, :, MAIN:]
    own_packed = pack(own[:, :, :MAIN], own_rest).astype(BF16)
    images[0, 0, 0] = own_packed[0]
    texts[0, 0, 0] = own_packed[1]
    pl.semaphore_wait(barrier, 13)

    def remote(src, dst, send, recv, device):
        return pltpu.make_async_remote_copy(
            src_ref=src,
            dst_ref=dst,
            send_sem=send_sems.at[send],
            recv_sem=recv,
            device_id=device,
            device_id_type=MESH,
        )

    def arrived(ref, recv):
        remote(ref, ref, 0, recv, partner).wait_recv()

    def left(ref, send):
        remote(ref, ref, send, text_core_recv.at[0], partner).wait_send()

    def spread(blocks, plane, send, recv, dz):
        for k in AROUND:
            remote(blocks.at[0, dz, 0], blocks.at[0, dz, k], send, recv.at[dz], plane[k]).start()

    def to_partner(blocks, plane_recv, send, core_recv, dz):
        arrived(blocks.at[0, dz, pl.ds(1, 3)], plane_recv.at[dz])
        remote(blocks.at[0, dz], blocks.at[1, dz], send, core_recv.at[dz], partner).start()

    def unpack_set(blocks, rests, lane, dz):
        rests[lane, dz] = unpack_rest(blocks[lane, dz].astype(F32)).astype(BF16)

    def partner_complete(blocks, rests, core_recv, dz):
        arrived(blocks.at[1, dz], core_recv.at[dz])
        unpack_set(blocks, rests, 1, dz)

    for k in (1, 2, 3):
        remote(texts.at[0, 0, 0], texts.at[0, k, 0], 0, text_z_recv.at[k], text_z[k]).start()
    for k in (1, 2, 3):
        remote(images.at[0, 0, 0], images.at[0, k, 0], 2, image_z_recv.at[k], image_z[k]).start()
    spread(texts, text_plane, 1, text_plane_recv, 0)
    spread(images, image_plane, 3, image_plane_recv, 0)
    for dz in (1, 2, 3):
        arrived(texts.at[0, dz, 0], text_z_recv.at[dz])
        spread(texts, text_plane, 1, text_plane_recv, dz)
    for dz in (1, 2, 3):
        arrived(images.at[0, dz, 0], image_z_recv.at[dz])
        spread(images, image_plane, 3, image_plane_recv, dz)
    for dz in range(4):
        to_partner(texts, text_plane_recv, 4, text_core_recv, dz)
    for dz in range(4):
        to_partner(images, image_plane_recv, 5, image_core_recv, dz)
        unpack_set(texts, texts_rest, 0, dz)
        if dz > 0:
            unpack_set(images, images_rest, 0, dz - 1)
    unpack_set(images, images_rest, 0, 3)

    scale, bias = scale_ref[()], bias_ref[()]
    half = 16 * ROWS
    across = ((1,), (1,))

    def flat(ref, lane):
        return ref[lane].reshape(half, ref.shape[-1])

    def logits_of(rows, cols, col_lane):
        products = dot(flat(rows[0], 0), flat(cols[0], col_lane), across)
        products = products + dot(flat(rows[1], 0), flat(cols[1], col_lane), across)
        return scale * products + bias

    def ids(shape):
        return [lax.broadcasted_iota(jnp.int32, shape, dim) for dim in (0, 1)]

    def other_coefficients(rows, cols):
        logits = logits_of(rows, cols, 1)
        col = ids(logits.shape)[1]
        return jnp.where(col % ROWS < USED, jax.nn.sigmoid(logits), 0.0).astype(BF16)

    own, other = slice(0, half), slice(half, 2 * half)
    all_images, all_texts = (images, images_rest), (texts, texts_rest)
    logits = logits_of(all_images, all_texts, 0)
    row, col = ids(logits.shape)
    held = jnp.logical_and(row % ROWS < USED, col % ROWS < USED)
    image_coefs[:, own] = jnp.where(held, jax.nn.sigmoid(logits), 0.0).astype(BF16)
    corner = (slice(0, ROWS), slice(0, LANES))
    logits = logits[corner]
    row, col = ids(logits.shape)
    pairs = jnp.where(row == col, -jax.nn.sigmoid(-logits), jax.nn.sigmoid(logits))
    image_coefs[corner] = jnp.where(held[corner], pairs, 0.0).astype(BF16)

    def returns(coefs, cols, places, terms, out, into, send, recv, plane):
        first = places[-1]
        factor = coefs[4 * ROWS * first : 4 * ROWS * (first + 2), :]
        main, rest = (
            dot(factor, ref[...].reshape(2 * half, ref.shape[-1]), ((1,), (0,))).reshape(8, ROWS, ref.shape[-1])
            for ref in cols
        )
        packed = pack(main, rest)
        for dz in places:
            blocks = packed[4 * (dz - first) : 4 * (dz - first + 1)]
            terms[dz] = blocks[0]
            out[dz] = blocks[1:4].astype(BF16)
            for k in AROUND:
                remote(out.at[dz, k - 1], into.at[dz, k - 1], send, recv.at[dz], plane[k]).start()

    def image_returns(places):
        returns(
            image_coefs, all_texts, places, image_terms, image_plane_out, image_plane_in, 6, image_back_recv, image_plane
        )

    def text_returns(places):
        returns(text_coefs, all_images, places, text_terms, text_plane_out, text_plane_in, 7, text_back_recv, text_plane)

    for dz in range(4):
        partner_complete(texts, texts_rest, text_core_recv, dz)
    image_coefs[:, other] = other_coefficients(all_images, all_texts)
    image_returns((3, 2))
    text_coefs[:, own] = image_coefs[:, own].astype(F32).T.astype(BF16)
    for dz in range(4):
        partner_complete(images, images_rest, image_core_recv, dz)
    text_coefs[:, other] = other_coefficients(all_texts, all_images)
    text_returns((3, 2))
    image_returns((1, 0))
    text_returns((1, 0))

    def summed(dz, terms, into, recv):
        arrived(into.at[dz], recv.at[dz])
        return terms[dz] + jnp.sum(into[dz].astype(F32), axis=0)

    def image_sum(dz):
        return summed(dz, image_terms, image_plane_in, image_back_recv)

    def text_sum(dz):
        return summed(dz, text_terms, text_plane_in, text_back_recv)

    def image_z_return(k):
        image_z_out[k - 1] = image_sum(k).astype(BF16)
        remote(image_z_out.at[k - 1], image_z_in.at[k - 1], 8, last_recv.at[0], image_z[k]).start()

    def text_z_return(k):
        text_z_out[k - 1] = text_sum(k).astype(BF16)
        remote(text_z_out.at[k - 1], text_z_in.at[k - 1], 9, last_recv.at[1], text_z[k]).start()

    image_z_return(3)
    image_z_return(2)
    text_z_return(3)
    text_z_return(2)
    image_z_return(1)
    text_z_return(1)
    for blocks, first in ((texts, 0), (images, 2)):
        left(blocks.at[0, 0, pl.ds(1, 3)], first)
        left(blocks.at[0, pl.ds(1, 3)], first + 1)
        left(blocks.at[0], first // 2 + 4)
    image_total = image_sum(0)
    text_total = text_sum(0)
    left(image_plane_out, 6)
    left(text_plane_out, 7)

    def finish(i, total, ref):
        arrived(ref, last_recv.at[i])
        total = scale * (total + jnp.sum(ref[...].astype(F32), axis=0))
        grads[i, :, :MAIN] = total
        grads[i, :, MAIN:] = unpack_rest(total[None])[0]
        grad, unit = grads[i, 0:USED], units[i, 0:USED]
        both_out[i] = recip[i] * (grad - unit * jnp.sum(unit * grad, axis=1, keepdims=True))

    finish(0, image_total, image_z_in)
    finish(1, text_total, text_z_in)
    left(image_z_out, 8)
    left(text_z_out, 9)


def shards(image_embed, text_embed, logit_scale, logit_bias):
    rows, width = image_embed.shape
    vmem = pl.BlockSpec(memory_space=pltpu.VMEM)
    hbm = pl.BlockSpec(memory_space=pltpu.HBM)
    out = jax.ShapeDtypeStruct((rows, width), F32)

    def half(*lead, columns=MAIN):
        return pltpu.VMEM((*lead, ROWS, columns), BF16)

    def full(*lead, columns=MAIN):
        return pltpu.VMEM((*lead, ROWS, columns), F32)

    def dma(*shape):
        return pltpu.SemaphoreType.DMA(shape)

    both = pl.pallas_call(
        kernel,
        out_shape=jax.ShapeDtypeStruct((2, rows, width), F32),
        in_specs=[pl.BlockSpec(memory_space=pltpu.SMEM)] * 2 + [hbm, hbm],
        out_specs=vmem,
        scratch_shapes=[
            pltpu.VMEM((2, rows, width), BF16),
            full(2, columns=width),
            full(2, columns=width),
            half(2, 4, 4),
            half(2, 4, 4),
            half(2, 4, 4, columns=REST),
            half(2, 4, 4, columns=REST),
            pltpu.VMEM((16 * ROWS, 32 * ROWS), BF16),
            pltpu.VMEM((16 * ROWS, 32 * ROWS), BF16),
            full(4),
            full(4),
            half(4, 3),
            half(4, 3),
            half(4, 3),
            half(4, 3),
            half(3),
            half(3),
            half(3),
            half(3),
            dma(2),
            dma(10),
            dma(4),
            dma(4),
            dma(4),
            dma(4),
            dma(4),
            dma(4),
            dma(4),
            dma(4),
            dma(2),
        ],
        compiler_params=pltpu.CompilerParams(
            collective_id=0, has_side_effects=True, vmem_limit_bytes=40 * 1024 * 1024
        ),
    )(
        logit_scale,
        logit_bias,
        pltpu.with_memory_space_constraint(image_embed, pltpu.HBM),
        pltpu.with_memory_space_constraint(text_embed, pltpu.HBM),
    )
    return both[0], both[1]


def solution(mesh):
    return jax.shard_map(
        shards,
        mesh=mesh,
        in_specs=(P(("blk", "grp"), None), P(("blk", "grp"), None), P(), P()),
        out_specs=(P(("blk", "grp"), None), P(("blk", "grp"), None)),
        check_vma=False,
    )
```
